512 devices in a mesh: dp: 16 (over x, z_hi, core), seq: 32 (over y, z_lo).
Axes of the slice: x: 4, y: 4, z: 16 (z_hi: 2, z_lo: 8; z = z_hi * 8 + z_lo), core: 2. Of those that a mesh axis runs over, the one named last changes fastest.
Arguments:
- latents: bfloat16 [16, 32, 256, 1152], P('dp', 'seq'), may hold values from -5 to 5
- caption: bfloat16 [16, 300, 1152], P('dp'), may hold values from -5 to 5
- caption_len: int32 [16], P('dp'), may hold values from 37 to 300, as said below
- modulation: float32 [16, 3, 1152], P('dp'), may hold values from -1 to 3
- cross_query: bfloat16 [1152, 576], P('seq')
- cross_keyval: bfloat16 [1152, 1152], P('seq')
- cross_output: bfloat16 [576, 1152], P('seq'), may hold values from -0.25 to 0.25
- time_qkv: bfloat16 [1152, 1728], P('seq')
- time_output: bfloat16 [576, 1152], P('seq'), may hold values from -0.25 to 0.25
- cotangent: bfloat16 [16, 32, 256, 1152], P('dp', 'seq'), may hold values from -6 to 6
Outputs:
- output: bfloat16 [16, 32, 256, 1152], P('dp', 'seq')
- grad_latents: bfloat16 [16, 32, 256, 1152], P('dp', 'seq')
- grad_modulation: float32 [16, 3, 1152], P('dp', None, 'seq')
- grad_time_output: float32 [576, 1152], P(None, 'seq')
The draws below stay inside these ranges and needn't reach their ends.
Inputs may be any that keep to these rules, and one draw needn't show every extreme that they name: `caption_len`: number of caption tokens in use for each clip; the slots from it on are padding.
All inputs are finite; a program needn't handle non-finite values.
Results may differ from the reference program's by a relative error of at most 0.035.
Values may be sent and summed in bfloat16 or wider, within the bound.
A program may use at most 64 MiB of HBM per device.

```python
import jax
import jax.numpy as jnp
from jax import lax

D = 1152
HEADS = 8
CAPTION = 300
PATCHES = 256
INNER = 576
CLIPS = 16
FRAMES = 32
TOKENS = 131072


def draw_latents(key, part):
    key = jax.random.fold_in(key, 1)
    first_key = jax.random.fold_in(key, 0)
    values = jax.random.normal(first_key, (CLIPS, FRAMES, PATCHES, D))
    return jnp.clip(values, -5.0, 5.0).astype(jnp.bfloat16)


def draw_caption(key, part):
    key = jax.random.fold_in(key, 2)
    first_key = jax.random.fold_in(key, 0)
    values = jax.random.normal(first_key, (CLIPS, CAPTION, D))
    return jnp.clip(values, -5.0, 5.0).astype(jnp.bfloat16)


def draw_caption_len(key, part):
    key = jax.random.fold_in(key, 3)
    first_key, second_key = jax.random.split(key, 2)
    values = jax.random.randint(first_key, (CLIPS,), CAPTION // 8, CAPTION + 1)
    chosen = jax.random.randint(second_key, (), 0, CLIPS)
    values = values.at[chosen].set(CAPTION)
    values = values.at[(chosen + 1) % CLIPS].set(CAPTION // 8)
    return values.astype(jnp.int32)


def draw_modulation(key, part):
    key = jax.random.fold_in(key, 4)
    first_key = jax.random.fold_in(key, 0)
    values = jnp.clip(0.5 * jax.random.normal(first_key, (CLIPS, 3, D)), -1.0, 1.0)
    return values.astype(jnp.float32)


def draw_cross_query(key, part):
    key = jax.random.fold_in(key, 5)
    values = jnp.clip(jax.random.normal(key, (D, INNER)), -4.0, 4.0) * D ** (-0.5)
    return values.astype(jnp.bfloat16)


def draw_cross_keyval(key, part):
    key = jax.random.fold_in(key, 6)
    first_key = jax.random.fold_in(key, 0)
    values = jnp.clip(jax.random.normal(first_key, (D, 2 * INNER)), -4.0, 4.0) * D ** (-0.5)
    return values.astype(jnp.bfloat16)


def draw_time_qkv(key, part):
    key = jax.random.fold_in(key, 7)
    first_key = jax.random.fold_in(key, 0)
    values = jnp.clip(jax.random.normal(first_key, (D, 3 * INNER)), -4.0, 4.0) * D ** (-0.5)
    return values.astype(jnp.bfloat16)


def with_spikes(entries, rng, source, target, shards_of, factor):
    def block_of(dim):
        return (jnp.arange(entries.shape[dim]) // (entries.shape[dim] // shards_of)).reshape((-1,) + (1,) * (entries.ndim - 1 - dim))

    first = jax.random.permutation(rng, shards_of)[block_of(target)]
    far = (block_of(target) + shards_of // 2) % shards_of
    return jnp.where((block_of(source) == first) | (block_of(source) == far), factor * entries, entries)


def block_scale(stream_key, shape, shards, low, high):
    loudness = 1.0
    for axis_at, blocks in shards:
        draws = jax.random.uniform(jax.random.fold_in(jax.random.fold_in(stream_key, 6), axis_at), (blocks,), jnp.float32, low / len(shards), high / len(shards))
        loudness = loudness * jnp.repeat(jnp.exp(draws), shape[axis_at] // blocks).reshape((-1,) + (1,) * (len(shape) - 1 - axis_at))
    return loudness


def centred(own_key, extent, deviation, bound, shards=(), kind=jnp.bfloat16):
    values = deviation * jax.random.normal(own_key, extent, jnp.float32)
    if shards:
        values = values * block_scale(own_key, extent, shards, -0.22, 0.18)
    return jnp.clip(values, -bound, bound).astype(kind)


def gaussian_with(stream_key, shape, spread, reach, cuts, heavy, kind=jnp.bfloat16):
    result = spread * jax.random.normal(stream_key, shape, jnp.float32)
    if cuts:
        result = result * block_scale(stream_key, shape, cuts, -0.22, 0.18)
    return jnp.clip(with_spikes(result, jax.random.fold_in(stream_key, 3), *heavy), -reach, reach).astype(kind)


def setup_inputs(seed: int = 0) -> dict:
    streams_of = jax.random.split(jax.random.key(seed), 11)
    latents = draw_latents(jax.random.fold_in(streams_of[10], 71), 0)
    caption = draw_caption(jax.random.fold_in(streams_of[10], 71), 0)
    caption_len = draw_caption_len(jax.random.fold_in(streams_of[10], 71), 0)
    modulation = draw_modulation(jax.random.fold_in(streams_of[10], 71), 0)
    cross_query = draw_cross_query(jax.random.fold_in(streams_of[10], 71), 0)
    cross_keyval = draw_cross_keyval(jax.random.fold_in(streams_of[10], 71), 0)
    cross_output = centred(streams_of[6], (INNER, D), INNER ** -0.5, 0.25, ((0, 32),))
    time_qkv = draw_time_qkv(jax.random.fold_in(streams_of[10], 71), 0)
    time_output = centred(streams_of[8], (INNER, D), INNER ** -0.5, 0.25, ((0, 32),))
    cotangent = gaussian_with(streams_of[9], (CLIPS, FRAMES, PATCHES, D), 1.0, 6.0, ((0, 16), (1, 32)), (1, 3, 32, 2.75))
    return dict(latents=latents, caption=caption, caption_len=caption_len, modulation=modulation, cross_query=cross_query, cross_keyval=cross_keyval, cross_output=cross_output, time_qkv=time_qkv, time_output=time_output, cotangent=cotangent)


eps_norm = 1e-06

def as_float(value):
    return value.astype(jnp.float32)

def to_low(value):
    return lax.optimization_barrier(value.astype(jnp.bfloat16))

def norm_rows(hidden):
    widened = as_float(hidden)
    center = widened - lax.optimization_barrier(jnp.mean(widened, axis=-1, keepdims=True))
    inv_std = lax.rsqrt(lax.optimization_barrier(jnp.mean(center * center, axis=-1, keepdims=True)) + eps_norm)
    return (center * inv_std, inv_std)

def norm_back(grad_norm, normed, inv_std):
    first_mean = lax.optimization_barrier(jnp.mean(grad_norm, axis=-1, keepdims=True))
    second_mean = lax.optimization_barrier(jnp.mean(grad_norm * normed, axis=-1, keepdims=True))
    return inv_std * (grad_norm - first_mean - normed * second_mean)

def cross_soft(query_heads, key_rows, length, head_scale):
    scores = jnp.einsum('rhe,che->hrc', as_float(query_heads), as_float(key_rows)) * head_scale
    valid = jnp.arange(key_rows.shape[0], dtype=jnp.int32) < length
    return jax.nn.softmax(jnp.where(valid, scores, -1e+30), axis=-1)

def split_heads(packed, index, inner_width):
    block = packed[..., index * inner_width:(index + 1) * inner_width]
    return as_float(block).reshape(block.shape[:-1] + (HEADS, inner_width // HEADS))

def time_soft(packed, inner_width):
    queries = split_heads(packed, 0, inner_width)
    key_rows = split_heads(packed, 1, inner_width)
    head_scale = (inner_width // HEADS) ** (-0.5)
    scores = jnp.einsum('fphe,gphe->phfg', queries, key_rows) * head_scale
    return (jax.nn.softmax(scores, axis=-1), queries, key_rows)

def time_forward(packed, inner_width):
    soft, queries, key_rows = time_soft(packed, inner_width)
    value_rows = split_heads(packed, 2, inner_width)
    mixed = jnp.einsum('phfg,gphe->fphe', as_float(to_low(soft)), value_rows)
    return to_low(mixed.reshape(mixed.shape[:2] + (inner_width,)))

def time_backward(packed, grad_mixed, inner_width):
    soft, queries, key_rows = time_soft(packed, inner_width)
    value_rows = split_heads(packed, 2, inner_width)
    head_scale = (inner_width // HEADS) ** (-0.5)
    grad_heads = as_float(grad_mixed).reshape(grad_mixed.shape[:2] + (HEADS, inner_width // HEADS))
    grad_soft = jnp.einsum('fphe,gphe->phfg', grad_heads, value_rows)
    grad_values = to_low(jnp.einsum('phfg,fphe->gphe', as_float(to_low(soft)), grad_heads))
    delta_rows = lax.optimization_barrier(jnp.sum(soft * grad_soft, axis=-1, keepdims=True))
    grad_scores = as_float(to_low(soft * (grad_soft - delta_rows) * head_scale))
    grad_queries = to_low(jnp.einsum('phfg,gphe->fphe', grad_scores, key_rows))
    grad_keys = to_low(jnp.einsum('phfg,fphe->gphe', grad_scores, queries))
    lead = grad_mixed.shape[:2] + (inner_width,)
    return jnp.concatenate([grad_queries.reshape(lead), grad_keys.reshape(lead), grad_values.reshape(lead)], axis=-1)

def one_clip(latent, caption_rows, length, mod_rows, grad_out, weights):
    cross_query, cross_keyval, cross_output, time_qkv, time_output = weights
    frames_all, patch_count, model_width = latent.shape
    inner_width = cross_query.shape[1]
    head_size = inner_width // HEADS
    head_scale = head_size ** (-0.5)
    row_count = frames_all * patch_count
    latent_rows = latent.reshape(row_count, model_width)
    queries = to_low(jnp.dot(latent_rows, cross_query, preferred_element_type=jnp.float32))
    keyval = to_low(jnp.dot(caption_rows, cross_keyval, preferred_element_type=jnp.float32))
    key_rows = keyval[:, :inner_width].reshape(-1, HEADS, head_size)
    value_rows = keyval[:, inner_width:].reshape(-1, HEADS, head_size)
    query_heads = queries.reshape(row_count, HEADS, head_size)
    cross_probs = cross_soft(query_heads, key_rows, length, head_scale)
    attended = jnp.einsum('hrc,che->rhe', as_float(to_low(cross_probs)), as_float(value_rows))
    attended = to_low(attended.reshape(row_count, inner_width))
    hidden = to_low(as_float(latent_rows) + jnp.dot(attended, cross_output, preferred_element_type=jnp.float32))
    normed, inv_std = norm_rows(hidden)
    shift_row = mod_rows[0]
    scale_row = mod_rows[1]
    gate_row = mod_rows[2]
    modded = to_low(normed * (1.0 + scale_row) + shift_row)
    packed = to_low(jnp.dot(modded, time_qkv, preferred_element_type=jnp.float32))
    packed = packed.reshape(frames_all, patch_count, 3 * inner_width)
    mixed = time_forward(packed, inner_width).reshape(row_count, inner_width)
    branch = jnp.dot(mixed, time_output, preferred_element_type=jnp.float32)
    output = to_low(as_float(hidden) + gate_row * branch)
    grad_rows = as_float(grad_out.reshape(row_count, model_width))
    grad_branch = to_low(gate_row * grad_rows)
    grad_weight = jnp.dot(mixed.T, grad_branch, preferred_element_type=jnp.float32)
    grad_mixed = to_low(jnp.dot(grad_branch, time_output.T, preferred_element_type=jnp.float32))
    grad_packed = time_backward(packed, grad_mixed.reshape(frames_all, patch_count, inner_width), inner_width)
    grad_packed = grad_packed.reshape(row_count, 3 * inner_width)
    grad_modded = jnp.dot(grad_packed, time_qkv.T, preferred_element_type=jnp.float32)
    grad_normterm = to_low(norm_back(grad_modded * (1.0 + scale_row), normed, inv_std))
    grad_hidden = to_low(grad_rows + as_float(grad_normterm))
    grad_attended = to_low(jnp.dot(grad_hidden, cross_output.T, preferred_element_type=jnp.float32))
    grad_cprobs = jnp.einsum('rhe,che->hrc', as_float(grad_attended.reshape(row_count, HEADS, head_size)), as_float(value_rows))
    delta_rows = lax.optimization_barrier(jnp.sum(cross_probs * grad_cprobs, axis=-1, keepdims=True))
    grad_cscores = to_low(cross_probs * (grad_cprobs - delta_rows) * head_scale)
    grad_queries = jnp.einsum('hrc,che->rhe', as_float(grad_cscores), as_float(key_rows))
    grad_queries = to_low(grad_queries.reshape(row_count, inner_width))
    grad_latent = to_low(as_float(grad_hidden) + jnp.dot(grad_queries, cross_query.T, preferred_element_type=jnp.float32))
    grad_mod = jnp.stack([lax.optimization_barrier(jnp.sum(grad_modded, axis=0)), lax.optimization_barrier(jnp.sum(grad_modded * normed, axis=0)), lax.optimization_barrier(jnp.sum(grad_rows * branch, axis=0))])
    grad_mod = grad_mod * row_count ** (-0.5)
    return (output.reshape(latent.shape), grad_latent.reshape(latent.shape), grad_mod, grad_weight)

def reference(latents, caption, caption_len, modulation, cross_query, cross_keyval, cross_output, time_qkv, time_output, cotangent):
    weights = (cross_query, cross_keyval, cross_output, time_qkv, time_output)

    def per_clip(items):
        return one_clip(items[0], items[1], items[2], items[3], items[4], weights)
    outputs, grads, mod_grads, weight_terms = lax.map(per_clip, (latents, caption, caption_len, modulation, cotangent))
    grad_time_output = lax.optimization_barrier(jnp.sum(weight_terms, axis=0)) * TOKENS ** (-0.5)
    return (outputs, grads, mod_grads, grad_time_output)
```

```python
import jax
import jax.numpy as jnp
from jax import lax
from jax.experimental import pallas as pl
from jax.experimental.pallas import tpu as pltpu
from jax.sharding import PartitionSpec as P

MESH = pl.DeviceIdType.MESH
F32 = jnp.float32
BF16 = jnp.bfloat16
HEADS = 8
HEAD = 72
INNER = HEADS * HEAD
WIDE = 640
MODEL = 1152
ROWS = 256
SLOTS = 384
SEQ = 32
EPS = 1e-6
NEG = -1e30
HEAD_SCALE = HEAD ** (-0.5)
RB, R0, R1, RM, R2 = range(5)
STAGED = {R0: 0, R1: 288, RM: 576, RB: 864, R2: 1008}
FIRST_BLOCK = {RB: 0, R0: 0, R1: 8, R2: 16, RM: 24}


def dot_nn(a, b):
    return lax.dot_general(a, b, (((1,), (0,)), ((), ())), preferred_element_type=F32)


def dot_nt(a, b):
    return lax.dot_general(a, b, (((1,), (1,)), ((), ())), preferred_element_type=F32)


def dot_tn(a, b):
    return lax.dot_general(a, b, (((0,), (0,)), ((), ())), preferred_element_type=F32)


def window(head):
    low = HEAD * head // 128 * 128
    high = -(-(HEAD * (head + 1)) // 128) * 128
    return low, high


def head_mask(head):
    low, high = window(head)
    lane = lax.broadcasted_iota(jnp.int32, (1, high - low), 1) + low
    return jnp.where((lane >= HEAD * head) & (lane < HEAD * (head + 1)), 1.0, 0.0).astype(BF16)


def kernel(
    query_shard,
    keyval_shard,
    cross_out_shard,
    qkv_shard,
    time_out_shard,
    latents,
    caption,
    length_ref,
    modulation,
    cotangent,
    out_ref,
    grad_latents,
    grad_mod,
    grad_weight,
    cols_a,
    cols_b,
    qkv_wide,
    pair_rows,
    z_wide_send,
    z_send,
    z_recv,
    z_wide,
    z_rows,
    own,
    keyval_wide,
    latent_rows,
    rows_wide,
    latent_recv,
    att_send,
    att_recv,
    wa,
    wb,
    cross_out,
    time_out,
    keys,
    values,
    queries,
    probs_c,
    acc,
    hidden_rows,
    gm_send,
    gm_recv,
    mix_send,
    mix_recv,
    term_send,
    term_recv,
    normed_ref,
    packed_ref,
    probs_t,
    grad_branch,
    gw_send,
    gw_core,
    gw_half,
    gw_x,
    gw_part,
    gw_y1,
    gw_part1,
    gw_y,
    gw_tile,
    gw_z,
    gw_red,
    gw_all,
    gw_last,
    mod_sum,
    mod_y,
    mod_tile,
    mod_z,
    zs_send,
    zs_recv,
    ring_send,
    a_recv,
    b_recv,
    core_send,
    core_recv,
    local_sem,
    all_send,
    all_recv,
    red_send,
    red_recv,
    core_part_recv,
):
    dp, s = lax.axis_index("dp"), lax.axis_index("seq")
    x, zh, c = dp // 4, (dp // 2) % 2, dp % 2
    y, zl = s // 8, s % 8
    z = zh * 8 + zl
    u = c * 4 + x

    def at(px, py, pz, pc):
        px, py, pz = lax.rem(px + 4, 4), lax.rem(py + 4, 4), lax.rem(pz + 16, 16)
        return (px * 4 + (pz // 8) * 2 + pc, py * 8 + lax.rem(pz, 8))

    def remote(src, dst, send, recv, device):
        return pltpu.make_async_remote_copy(
            src_ref=src, dst_ref=dst, send_sem=send, recv_sem=recv, device_id=device, device_id_type=MESH
        )

    def wait_bytes(ref, sem):
        pltpu.make_async_copy(ref, ref, sem).wait()

    barrier = pltpu.get_barrier_semaphore()

    def greet(i, carry):
        pl.semaphore_signal(barrier, inc=1, device_id=(dp, lax.rem(s + i, SEQ)), device_id_type=MESH)
        return carry

    lax.fori_loop(1, SEQ, greet, 0)
    for i in range(8):
        pl.semaphore_signal(barrier, inc=1, device_id=at(x, y, (1 - zh) * 8 + i, c), device_id_type=MESH)
    for i in range(1, 8):
        peer = lax.rem(x * 2 + c + i, 8)
        pl.semaphore_signal(barrier, inc=1, device_id=at(peer // 2, y, z, peer % 2), device_id_type=MESH)

    cols_a[...] = jnp.zeros_like(cols_a)
    qkv_wide[...] = jnp.zeros_like(qkv_wide)
    z_wide_send[...] = jnp.zeros_like(z_wide_send)
    cols_a[0:36, 0:1152] = keyval_shard[...].astype(F32)
    cols_a[0:36, 1152:1728] = query_shard[...].astype(F32)
    qkv_wide[0:36, 0:1728] = qkv_shard[...].astype(F32)
    turned = pltpu.roll(qkv_wide[...], 64, 1)
    cols_a[:, 1664:1792] += turned[:, 0:128]
    cols_a[:, 1792:3456] = turned[:, 128:1792]
    cols_b[0:18, 0:128] = time_out_shard[:, 1024:1152].astype(F32)
    cols_b[0:18, 128:1280] = cross_out_shard[...].astype(F32)
    cols_b[0:18, 1280:2304] = time_out_shard[:, 0:1024].astype(F32)

    def block_of(first):
        return pl.ds(pl.multiple_of(first * 128, 128), 128)

    z_wide_send[0:36, :] = cols_a[0:36, block_of(u)]
    z_wide_send[36:72, :] = cols_a[0:36, block_of(8 + u)]
    z_wide_send[128:164, :] = cols_a[0:36, block_of(16 + u)]
    z_wide_send[108:126, :] = cols_b[0:18, block_of(10 + u)]
    pair = lax.max(u - 3, 0)
    pair_rows[0:18, :] = cols_b[0:18, block_of(2 * pair)]
    pair_rows[18:36, :] = cols_b[0:18, block_of(2 * pair + 1)]
    z_wide_send[72:108, :] = jnp.where(u < 3, cols_a[0:36, block_of(lax.min(24 + u, 26))], pair_rows[0:36, :])
    z_send[...] = z_wide_send[...].astype(BF16)

    pl.semaphore_wait(barrier, 31 + 8 + 7)

    def along_z(part, first, count, step):
        rows = pl.ds(first, count)
        remote(
            z_send.at[rows], z_recv.at[zl, rows], zs_send.at[part], zs_recv.at[part], at(x, y, z + step, c)
        ).start()

    for part, first, cut, count in ((0, 0, 64, 128), (1, 128, 32, 48)):
        for step in (1, -1, 2, -2, 3, -3):
            along_z(part, first, count, step)
        along_z(part, first, cut, 4)
        along_z(part, first + cut, count - cut, -4)
    z_recv[pl.ds(zl, 1)] = z_send[...].reshape(1, 176, 128)

    shift_row = modulation[0]
    scale_row = 1.0 + modulation[1]
    gate_row = modulation[2]
    grad_branch[...] = (gate_row * cotangent[...].astype(F32)).astype(BF16)
    latent_rows[...] = latents[...].astype(F32).reshape(ROWS, MODEL).astype(BF16)
    keys[...] = jnp.zeros_like(keys)
    values[...] = jnp.zeros_like(values)
    keyval_wide[296:304, :] = jnp.zeros((8, MODEL), F32)
    rows_wide[...] = jnp.zeros_like(rows_wide)
    cross_out[INNER:WIDE, :] = jnp.zeros((WIDE - INNER, MODEL), BF16)
    time_out[INNER:WIDE, :] = jnp.zeros((WIDE - INNER, MODEL), BF16)
    mod_sum[...] = jnp.zeros_like(mod_sum)

    def place(i, j):
        px = lax.rem(x + i * (1 - c) + j * c + 4, 4)
        py = lax.rem(y + i * c + j * (1 - c) + 4, 4)
        return px, py

    def neighbour(i, j):
        px, py = place(i, j)
        return at(px, py, z, c)

    def piece(k, i, j, half=None):
        px, py = place(i, j)
        count = 144 if k == RB else 288
        start, size = 0, count
        if half is not None:
            cut = 80 if k == RB else 144
            start, size = (0, cut) if half == 0 else (cut, count - cut)
        buf = wb if k == RB else wa
        row = pl.multiple_of(py * count + start, 16)
        col = pl.multiple_of((FIRST_BLOCK[k] + 4 * c + px) * 128, 128)
        return buf.at[pl.ds(row, size), pl.ds(col, 128)]

    def own_piece(k):
        return own.at[pl.ds(STAGED[k], 144 if k == RB else 288)]

    def pieces_like(k, count):
        return wa.at[pl.ds(0, 144 if k == RB else 288), pl.ds(0, 128 * count)]

    def halves_like(k, half, count):
        size = (80 if half == 0 else 64) if k == RB else 144
        return wa.at[pl.ds(0, size), pl.ds(0, 128 * count)]

    def core_part(k, core):
        buf = wb if k == RB else wa
        col = pl.multiple_of((FIRST_BLOCK[k] + 4 * core) * 128, 128)
        return buf.at[:, pl.ds(col, 512)]

    def stage1(k):
        pltpu.make_async_copy(own_piece(k), piece(k, 0, 0), local_sem.at[k]).start()
        for side, step in ((0, 1), (1, -1)):
            remote(own_piece(k), piece(k, 0, 0), ring_send.at[k], a_recv.at[k, side], neighbour(step, 0)).start()

    def stage2(k):
        for side, step in ((0, 1), (1, -1)):
            wait_bytes(piece(k, -step, 0), a_recv.at[k, side])
            ref = piece(k, -step, 0, half=side)
            remote(ref, ref, ring_send.at[k], a_recv.at[k, 2 + side], neighbour(step, 0)).start()
        for i in (0, -1, 1):
            for side, step in ((0, 1), (1, -1)):
                src = own_piece(k) if i == 0 else piece(k, i, 0)
                remote(src, piece(k, i, 0), ring_send.at[k], b_recv.at[k, side], neighbour(0, step)).start()

    def stage3(k):
        for side in (0, 1):
            wait_bytes(halves_like(k, side, 1), a_recv.at[k, 2 + side])
        for side, step in ((0, 1), (1, -1)):
            ref = piece(k, 2, 0)
            remote(ref, ref, ring_send.at[k], b_recv.at[k, side], neighbour(0, step)).start()
        pltpu.make_async_copy(own_piece(k), piece(k, 0, 0), local_sem.at[k]).wait()
        to_core(k, [(i, 0) for i in (0, -1, 1, 2)])

    def stage4(k):
        for side, step in ((0, 1), (1, -1)):
            wait_bytes(pieces_like(k, 4), b_recv.at[k, side])
            for i in (0, -1, 1, 2):
                ref = piece(k, i, -step, half=side)
                remote(ref, ref, ring_send.at[k], b_recv.at[k, 2 + side], neighbour(0, step)).start()
        to_core(k, [(i, j) for j in (-1, 1) for i in (0, -1, 1, 2)])

    def to_core(k, places):
        for i, j in places:
            ref = piece(k, i, j)
            remote(ref, ref, core_send.at[k], core_recv.at[k], at(x, y, z, 1 - c)).start()

    def stage5(k):
        for side in (0, 1):
            wait_bytes(halves_like(k, side, 4), b_recv.at[k, 2 + side])
        to_core(k, [(i, 2) for i in (0, -1, 1, 2)])

    def stage6(k):
        wait_bytes(core_part(k, 1 - c), core_recv.at[k])

    def exchange(src, dst, index):
        def send(i, carry):
            d = lax.rem(s + i, SEQ)
            remote(src.at[d], dst.at[s], all_send.at[index], all_recv.at[index], (dp, d)).start()
            return carry

        lax.fori_loop(1, SEQ, send, 0)
        dst[pl.ds(s, 1)] = src[pl.ds(s, 1)]

    def arrived(dst, index):
        wait_bytes(dst.at[pl.ds(0, 31)], all_recv.at[index])

    def unpack_pairs():
        for slot in range(5):
            col = (27 + slot) * 128
            for half in range(2):
                block = 2 * slot + half
                for part in range(4):
                    rows = slice(288 * part + 144 * half, 288 * part + 144 * half + 144)
                    target = slice(144 * part, 144 * part + 144)
                    if block == 0:
                        time_out[target, 1024:1152] = wa[rows, col : col + 128]
                    else:
                        cross_out[target, (block - 1) * 128 : block * 128] = wa[rows, col : col + 128]

    def put_rows(recv):
        rows_wide[:, 0:INNER] = recv[...].astype(F32).reshape(ROWS, INNER).astype(BF16)

    order = (R0, R1, RM, RB, R2)
    early = (R0, R1, RM)
    late = (RB, R2)
    wait_bytes(z_recv.at[pl.ds(0, 7), pl.ds(0, 128)], zs_recv.at[0])
    z_wide[:, 0:128, :] = z_recv[:, 0:128, :].astype(F32)

    def spread(k, first):
        base = STAGED[k]
        for j in range(8):
            z_rows[base + 36 * j : base + 36 * j + 36, :] = z_wide[j, first : first + 36, :]
        own[base : base + 288, :] = z_rows[base : base + 288, :].astype(BF16)

    spread(R0, 0)
    stage1(R0)
    spread(R1, 36)
    stage1(R1)
    for j in range(8):
        z_rows[576 + 36 * j : 612 + 36 * j, :] = z_wide[j, 72:108, :]
        z_rows[1296 + 18 * j : 1314 + 18 * j, :] = z_wide[j, 72:90, :]
        z_rows[1440 + 18 * j : 1458 + 18 * j, :] = z_wide[j, 90:108, :]
        z_rows[864 + 18 * j : 882 + 18 * j, :] = z_wide[j, 108:126, :]
    own[576:864, :] = jnp.where(u < 3, z_rows[576:864, :], z_rows[1296:1584, :]).astype(BF16)
    own[864:1008, :] = z_rows[864:1008, :].astype(BF16)
    stage1(RM)
    exchange(latents, latent_recv, 1)
    wait_bytes(z_recv.at[pl.ds(0, 7), pl.ds(128, 48)], zs_recv.at[1])
    z_wide[:, 128:176, :] = z_recv[:, 128:176, :].astype(F32)
    spread(R2, 128)
    for stage in (stage2, stage3, stage4, stage5):
        for k in early:
            stage(k)
    for k in late:
        stage1(k)

    stage6(R0)
    stage6(R1)
    keyval_wide[0:300, :] = dot_nn(caption[...], wa[:, 0:1152])
    keys[0:304, 0:INNER] = keyval_wide[:, 0:INNER].astype(BF16)
    turned = pltpu.roll(keyval_wide[:, 512:1152], 576, 1)
    values[0:304, 0:INNER] = turned[:, 0:INNER].astype(BF16)
    for k in late:
        stage2(k)
    queries[...] = dot_nn(latent_rows[...], wa[:, 1152:1792]).astype(BF16)
    for k in late:
        stage3(k)

    slot = lax.broadcasted_iota(jnp.int32, (1, SLOTS), 1)
    bias = jnp.where(slot < length_ref[0], 0.0, NEG)
    acc[...] = jnp.zeros_like(acc)
    for head in range(HEADS):
        low, high = window(head)
        mask = head_mask(head)
        scores = dot_nt(queries[:, low:high], keys[:, low:high] * mask) * HEAD_SCALE + bias
        weight = jnp.exp(scores - jnp.max(scores, axis=1, keepdims=True))
        soft = weight / jnp.sum(weight, axis=1, keepdims=True)
        probs_c[head] = soft
        acc[:, low:high] += dot_nn(soft.astype(BF16), values[:, low:high] * mask)
    attended = acc[...]
    att_send[...] = attended[:, 0:INNER].reshape(SEQ, 8, INNER).astype(BF16)
    exchange(att_send, att_recv, 4)
    for stage in (stage4, stage5):
        for k in late:
            stage(k)
    stage6(RM)
    unpack_pairs()
    hidden_rows[...] = (
        latent_rows[...].astype(F32) + dot_nn(attended.astype(BF16), cross_out[...])
    ).astype(BF16)
    stage6(RB)
    time_out[0:INNER, 0:1024] = wb[...]
    grad_mixed = dot_nt(grad_branch[...], time_out[...])
    gm_send[...] = grad_mixed[:, 0:INNER].reshape(SEQ, 8, INNER).astype(BF16)
    exchange(gm_send, gm_recv, 0)
    stage6(R2)
    arrived(latent_recv, 1)
    arrived(att_recv, 4)

    put_rows(att_recv)
    latent_patch = latent_recv[...].astype(F32).reshape(ROWS, MODEL)
    rows = (latent_patch + dot_nn(rows_wide[...], cross_out[...])).astype(BF16).astype(F32)
    center = rows - jnp.mean(rows, axis=1, keepdims=True)
    inv_std = lax.rsqrt(jnp.mean(center * center, axis=1, keepdims=True) + EPS)
    normed_ref[...] = center * inv_std
    modded = (normed_ref[...] * scale_row + shift_row).astype(BF16)
    packed = dot_nn(modded, wa[:, 1664:3456])
    packed_ref[0] = pltpu.roll(packed[:, 0:640], 576, 1).astype(BF16)
    packed_ref[1] = packed[:, 640:1280].astype(BF16)
    packed_ref[2] = pltpu.roll(packed[:, 1152:1792], 576, 1).astype(BF16)
    same = (
        lax.broadcasted_iota(jnp.int32, (ROWS, ROWS), 0) % 8 == lax.broadcasted_iota(jnp.int32, (ROWS, ROWS), 1) % 8
    )
    acc[...] = jnp.zeros_like(acc)
    for head in range(HEADS):
        low, high = window(head)
        mask = head_mask(head)
        scores = dot_nt(packed_ref[0, :, low:high], packed_ref[1, :, low:high] * mask) * HEAD_SCALE
        scores = jnp.where(same, scores, NEG)
        weight = jnp.exp(scores - jnp.max(scores, axis=1, keepdims=True))
        soft = weight / jnp.sum(weight, axis=1, keepdims=True)
        probs_t[head] = soft
        acc[:, low:high] += dot_nn(soft.astype(BF16), packed_ref[2, :, low:high] * mask)
    mix_send[...] = acc[:, 0:INNER].reshape(SEQ, 8, INNER).astype(BF16)
    exchange(mix_send, mix_recv, 2)

    arrived(gm_recv, 0)
    put_rows(gm_recv)
    parts = [[None] * 5 for _ in range(3)]

    def add_window(store, low, high, value):
        for block in range(low // 128, high // 128):
            piece_value = value[:, block * 128 - low : block * 128 - low + 128]
            store[block] = piece_value if store[block] is None else store[block] + piece_value

    for head in range(HEADS):
        low, high = window(head)
        mask = head_mask(head)
        soft = probs_t[head]
        grad_head = rows_wide[:, low:high] * mask
        grad_soft = dot_nt(grad_head, packed_ref[2, :, low:high])
        delta = jnp.sum(soft * grad_soft, axis=1, keepdims=True)
        grad_scores = (soft * (grad_soft - delta) * HEAD_SCALE).astype(BF16)
        add_window(parts[0], low, high, dot_nn(grad_scores, packed_ref[1, :, low:high] * mask))
        add_window(parts[1], low, high, dot_tn(grad_scores, packed_ref[0, :, low:high] * mask))
        add_window(parts[2], low, high, dot_tn(soft.astype(BF16), grad_head))
    grad_q, grad_k, grad_v = (jnp.concatenate(store, axis=1) for store in parts)
    grad_q = pltpu.roll(grad_q, 64, 1)
    grad_v = pltpu.roll(grad_v, 64, 1)
    grad_packed = jnp.concatenate(
        [grad_q, grad_k[:, 0:512], grad_k[:, 512:640] + grad_v[:, 0:128], grad_v[:, 128:640]], axis=1
    ).astype(BF16)
    grad_modded = dot_nt(grad_packed, wa[:, 1664:3456])
    mod_sum[0:1, 0:MODEL] = jnp.sum(grad_modded, axis=0, keepdims=True)
    mod_sum[1:2, 0:MODEL] = jnp.sum(grad_modded * normed_ref[...], axis=0, keepdims=True)
    grad_norm = grad_modded * scale_row
    first_mean = jnp.mean(grad_norm, axis=1, keepdims=True)
    second_mean = jnp.mean(grad_norm * normed_ref[...], axis=1, keepdims=True)
    term = inv_std * (grad_norm - first_mean - normed_ref[...] * second_mean)
    term_send[...] = term.reshape(SEQ, 8, MODEL).astype(BF16)
    exchange(term_send, term_recv, 3)

    arrived(mix_recv, 2)
    put_rows(mix_recv)
    mixed = rows_wide[...]
    partial = dot_tn(mixed, grad_branch[...])
    gw_send[...] = partial[0:INNER, :].reshape(72, 8, MODEL).astype(BF16)
    for i in (2, 1, 3, 0):
        part = lax.rem(x + i, 4)
        remote(
            gw_send.at[pl.ds(36 * (1 - c) + 9 * part, 9)],
            gw_core.at[pl.ds(9 * part, 9)],
            red_send.at[0],
            core_part_recv.at[part],
            at(x, y, z, 1 - c),
        ).start()
    branch = dot_nn(mixed, time_out[...])
    out_ref[...] = (hidden_rows[...].astype(F32) + gate_row * branch).astype(BF16)
    mod_sum[2:3, 0:MODEL] = jnp.sum(cotangent[...].astype(F32) * branch, axis=0, keepdims=True)
    for i in range(1, 4):
        remote(mod_sum, mod_y.at[i - 1], red_send.at[6], red_recv.at[6], at(x, y + i, z, c)).start()

    for i in (2, 1, 3, 0):
        part = lax.rem(x + i, 4)
        rows9 = pl.ds(9 * part, 9)
        wait_bytes(gw_core.at[rows9], core_part_recv.at[part])
        gw_half[rows9] = (
            gw_send[pl.ds(36 * c + 9 * part, 9)].astype(F32) + gw_core[rows9].astype(F32)
        ).astype(BF16)
        if i:

            @pl.when(c == 0)
            def _():
                remote(
                    gw_half.at[rows9], gw_x.at[i - 1], red_send.at[1], red_recv.at[1], at(part, y, z, c)
                ).start()

    own_cols = pl.ds(pl.multiple_of(256 * y, 128), 384)
    own_rows = pl.ds(9 * x, 9)

    def total_of(mine, others):
        total = mine.astype(F32)
        for i in range(3):
            total = total + others[i].astype(F32)
        return total.astype(BF16)

    def to_y(source, target, send, recv):
        for i in (2, 1, 3):
            to = lax.rem(y + i, 4)
            cols = pl.ds(pl.multiple_of(256 * to, 128), 384)
            remote(source.at[:, :, cols], target.at[i - 1], send, recv, at(x, to, z, c)).start()

    @pl.when(c == 1)
    def _():
        to_y(gw_half, gw_y1, red_send.at[1], red_recv.at[1])

    wait_bytes(mod_y, red_recv.at[6])
    mod_tile[...] = mod_sum[...] + mod_y[0] + mod_y[1] + mod_y[2]
    for i in range(1, 8):
        to = lax.rem(zl + i, 8)
        block = (36 * (8 * y + to)) // 128
        col = pl.multiple_of(block * 128, 128)
        remote(
            mod_tile.at[:, pl.ds(col, 256)], mod_z.at[i - 1], red_send.at[7], red_recv.at[7], (dp, 8 * y + to)
        ).start()

    @pl.when(c == 0)
    def _():
        wait_bytes(gw_x, red_recv.at[1])
        gw_part[...] = total_of(gw_half[own_rows], gw_x)
        to_y(gw_part, gw_y, red_send.at[2], red_recv.at[2])
        wait_bytes(gw_y, red_recv.at[2])
        gw_tile[...] = total_of(gw_part[:, :, own_cols], gw_y)

    @pl.when(c == 1)
    def _():
        wait_bytes(gw_y1, red_recv.at[1])
        gw_part1[...] = total_of(gw_half[:, :, own_cols], gw_y1)
        for i in (2, 1, 3):
            to = lax.rem(x + i, 4)
            remote(
                gw_part1.at[pl.ds(9 * to, 9)], gw_y.at[i - 1], red_send.at[2], red_recv.at[2], at(to, y, z, c)
            ).start()
        wait_bytes(gw_y, red_recv.at[2])
        gw_tile[...] = total_of(gw_part1[own_rows], gw_y)

    for group in range(9):

        @pl.when(z != group)
        def _():
            remote(
                gw_tile.at[group], gw_z.at[z], red_send.at[3], red_recv.at[3], at(x, y, jnp.int32(group), c)
            ).start()

    arrived(term_recv, 3)
    grad_hidden = (
        cotangent[...].astype(F32) + term_recv[...].astype(F32).reshape(ROWS, MODEL)
    ).astype(BF16)
    grad_attended = dot_nt(grad_hidden, cross_out[...]).astype(BF16)
    acc[...] = jnp.zeros_like(acc)

    def back(head):
        low, high = window(head)
        mask = head_mask(head)
        soft = probs_c[head]
        grad_soft = dot_nt(grad_attended[:, low:high], values[:, low:high] * mask)
        delta = jnp.sum(soft * grad_soft, axis=1, keepdims=True)
        grad_scores = (soft * (grad_soft - delta) * HEAD_SCALE).astype(BF16)
        acc[:, low:high] += dot_nn(grad_scores, keys[:, low:high] * mask)

    @pl.when(z < 9)
    def _():
        wait_bytes(gw_z.at[pl.ds(0, 15)], red_recv.at[3])
        gw_z[pl.ds(z, 1)] = gw_tile[pl.ds(z, 1)]
        total = jnp.sum(gw_z[...].astype(F32), axis=0)
        for place_z in range(8):
            turned = pltpu.roll(total, 384 - (32 * y + 36 * place_z), 1)
            gw_red[place_z] = turned[:, 0:128].astype(BF16)
        gw_all[pl.ds(z, 1)] = gw_red[pl.ds(zl, 1)]

        def send(i, carry):
            remote(
                gw_red.at[lax.rem(zl + i, 8)], gw_all.at[z], red_send.at[4], red_recv.at[4], at(x, y, z + i, c)
            ).start()
            return carry

        lax.fori_loop(1, 16, send, 0)

    for head in range(4):
        back(head)

    @pl.when(z < 9)
    def _():
        wait_bytes(gw_all.at[pl.ds(0, 8)], red_recv.at[4])

    @pl.when(z >= 9)
    def _():
        wait_bytes(gw_all, red_recv.at[4])

    gw_last[pl.ds(u, 1)] = gw_all[...].reshape(1, 9, 8, 128)
    for i in range(1, 8):
        peer = lax.rem(x * 2 + c + i, 8)
        remote(
            gw_all, gw_last.at[u], red_send.at[5], red_recv.at[5], at(peer // 2, y, z, peer % 2)
        ).start()

    for head in range(4, HEADS):
        back(head)
    grad_latents[...] = (
        grad_hidden.astype(F32) + dot_nt(acc[...].astype(BF16), wa[:, 1152:1792])
    ).astype(BF16)

    wait_bytes(mod_z, red_recv.at[7])
    block = (36 * s) // 128
    mod_total = mod_tile[:, pl.ds(pl.multiple_of(block * 128, 128), 256)]
    for i in range(7):
        mod_total = mod_total + mod_z[i]
    mod_total = pltpu.roll(mod_total, lax.rem(256 - (36 * s - 128 * block), 256), 1)
    for i in range(3):
        grad_mod[i] = mod_total[i : i + 1, 0:36] * (SEQ * ROWS) ** (-0.5)

    wait_bytes(gw_last.at[pl.ds(0, 7)], red_recv.at[5])
    total = jnp.transpose(gw_last[...].astype(F32).reshape(INNER, 128))
    grad_weight[...] = total[0:36, :] * (SEQ * ROWS * 16) ** (-0.5)

    wait_bytes(z_recv.at[pl.ds(0, 7), pl.ds(0, 128)], zs_send.at[0])
    wait_bytes(z_recv.at[pl.ds(0, 7), pl.ds(128, 48)], zs_send.at[1])
    for k in order:
        if k == RB:
            wait_bytes(wa.at[pl.ds(0, 144), pl.ds(0, 128 * 15)], ring_send.at[k])
        else:
            wait_bytes(pieces_like(k, 15), ring_send.at[k])
        wait_bytes(core_part(k, c), core_send.at[k])
    for index, ref in ((0, gm_recv), (1, latent_recv), (2, mix_recv), (3, term_recv), (4, att_recv)):
        wait_bytes(ref.at[pl.ds(0, 31)], all_send.at[index])
    wait_bytes(gw_core, red_send.at[0])
    wait_bytes(gw_y, red_send.at[2])

    @pl.when(c == 0)
    def _():
        wait_bytes(gw_x, red_send.at[1])

    @pl.when(c == 1)
    def _():
        wait_bytes(gw_y1, red_send.at[1])


    @pl.when(z < 9)
    def _():
        wait_bytes(gw_z.at[pl.ds(0, 8)], red_send.at[3])
        wait_bytes(gw_z.at[pl.ds(0, 15), :, pl.ds(0, 128)], red_send.at[4])

    @pl.when(z >= 9)
    def _():
        wait_bytes(gw_z.at[pl.ds(0, 9)], red_send.at[3])

    wait_bytes(gw_last.at[pl.ds(0, 7)], red_send.at[5])
    wait_bytes(mod_y, red_send.at[6])
    wait_bytes(mod_z, red_send.at[7])


def body(
    latents,
    caption,
    caption_len,
    modulation,
    cross_query,
    cross_keyval,
    cross_output,
    time_qkv,
    time_output,
    cotangent,
):
    vmem = pl.BlockSpec(memory_space=pltpu.VMEM)
    sems = pltpu.SemaphoreType.DMA
    out, grad_in, grad_mod, grad_w = pl.pallas_call(
        kernel,
        out_shape=(
            jax.ShapeDtypeStruct((ROWS, MODEL), BF16),
            jax.ShapeDtypeStruct((ROWS, MODEL), BF16),
            jax.ShapeDtypeStruct((3, 1, 36), F32),
            jax.ShapeDtypeStruct((36, INNER), F32),
        ),
        in_specs=[vmem] * 7 + [pl.BlockSpec(memory_space=pltpu.SMEM)] + [vmem] * 2,
        out_specs=(vmem,) * 4,
        scratch_shapes=[
            pltpu.VMEM((40, 3456), F32),
            pltpu.VMEM((24, 2304), F32),
            pltpu.VMEM((40, 1792), F32),
            pltpu.VMEM((40, 128), F32),
            pltpu.VMEM((176, 128), F32),
            pltpu.VMEM((176, 128), BF16),
            pltpu.VMEM((8, 176, 128), BF16),
            pltpu.VMEM((8, 176, 128), F32),
            pltpu.VMEM((1584, 128), F32),
            pltpu.VMEM((1296, 128), BF16),
            pltpu.VMEM((304, MODEL), F32),
            pltpu.VMEM((ROWS, MODEL), BF16),
            pltpu.VMEM((ROWS, WIDE), BF16),
            pltpu.VMEM((SEQ, 8, MODEL), BF16),
            pltpu.VMEM((SEQ, 8, INNER), BF16),
            pltpu.VMEM((SEQ, 8, INNER), BF16),
            pltpu.VMEM((MODEL, 4096), BF16),
            pltpu.VMEM((INNER, 1024), BF16),
            pltpu.VMEM((WIDE, MODEL), BF16),
            pltpu.VMEM((WIDE, MODEL), BF16),
            pltpu.VMEM((SLOTS, WIDE), BF16),
            pltpu.VMEM((SLOTS, WIDE), BF16),
            pltpu.VMEM((ROWS, WIDE), BF16),
            pltpu.VMEM((HEADS, ROWS, SLOTS), F32),
            pltpu.VMEM((ROWS, WIDE), F32),
            pltpu.VMEM((ROWS, MODEL), BF16),
            pltpu.VMEM((SEQ, 8, INNER), BF16),
            pltpu.VMEM((SEQ, 8, INNER), BF16),
            pltpu.VMEM((SEQ, 8, INNER), BF16),
            pltpu.VMEM((SEQ, 8, INNER), BF16),
            pltpu.VMEM((SEQ, 8, MODEL), BF16),
            pltpu.VMEM((SEQ, 8, MODEL), BF16),
            pltpu.VMEM((ROWS, MODEL), F32),
            pltpu.VMEM((3, ROWS, WIDE), BF16),
            pltpu.VMEM((HEADS, ROWS, ROWS), F32),
            pltpu.VMEM((ROWS, MODEL), BF16),
            pltpu.VMEM((72, 8, MODEL), BF16),
            pltpu.VMEM((36, 8, MODEL), BF16),
            pltpu.VMEM((36, 8, MODEL), BF16),
            pltpu.VMEM((3, 9, 8, MODEL), BF16),
            pltpu.VMEM((9, 8, MODEL), BF16),
            pltpu.VMEM((3, 36, 8, 384), BF16),
            pltpu.VMEM((36, 8, 384), BF16),
            pltpu.VMEM((3, 9, 8, 384), BF16),
            pltpu.VMEM((9, 8, 384), BF16),
            pltpu.VMEM((16, 8, 384), BF16),
            pltpu.VMEM((8, 8, 128), BF16),
            pltpu.VMEM((9, 8, 128), BF16),
            pltpu.VMEM((8, 9, 8, 128), BF16),
            pltpu.VMEM((8, 1280), F32),
            pltpu.VMEM((3, 8, 1280), F32),
            pltpu.VMEM((8, 1280), F32),
            pltpu.VMEM((7, 8, 256), F32),
            sems((2,)),
            sems((2,)),
            sems((5,)),
            sems((5, 4)),
            sems((5, 4)),
            sems((5,)),
            sems((5,)),
            sems((5,)),
            sems((5,)),
            sems((5,)),
            sems((8,)),
            sems((8,)),
            sems((4,)),
        ],
        compiler_params=pltpu.CompilerParams(
            collective_id=0, has_side_effects=True, vmem_limit_bytes=60 * 2**20
        ),
    )(
        cross_query,
        cross_keyval,
        cross_output,
        time_qkv,
        time_output,
        latents.reshape(SEQ, 8, MODEL),
        caption[0],
        caption_len,
        jnp.swapaxes(modulation, 0, 1),
        cotangent.reshape(ROWS, MODEL),
    )
    return (
        out.reshape(latents.shape),
        grad_in.reshape(latents.shape),
        jnp.swapaxes(grad_mod, 0, 1),
        jnp.swapaxes(grad_w, 0, 1),
    )


def solution(mesh):
    placed = (
        P("dp", "seq", None, None),
        P("dp", None, None),
        P("dp"),
        P("dp", None, None),
        P("seq", None),
        P("seq", None),
        P("seq", None),
        P("seq", None),
        P("seq", None),
        P("dp", "seq", None, None),
    )
    return jax.shard_map(
        body,
        mesh=mesh,
        in_specs=placed,
        out_specs=(
            P("dp", "seq", None, None),
            P("dp", "seq", None, None),
            P("dp", None, "seq"),
            P(None, "seq"),
        ),
        check_vma=False,
    )
```

```python
import jax
import jax.numpy as jnp
from jax import lax
from jax.experimental import pallas as pl
from jax.experimental.pallas import tpu as pltpu
from jax.sharding import PartitionSpec as P

MESH = pl.DeviceIdType.MESH
F32 = jnp.float32
BF16 = jnp.bfloat16
HEADS = 8
HEAD = 72
INNER = HEADS * HEAD
WIDE = 640
MODEL = 1152
ROWS = 256
SLOTS = 384
SEQ = 32
EPS = 1e-6
NEG = -1e30
HEAD_SCALE = HEAD ** (-0.5)
RB, R0, R1, RM, R2 = range(5)
STAGED = {R0: 0, R1: 288, RM: 576, RB: 864, R2: 1008}
FIRST_BLOCK = {RB: 0, R0: 0, R1: 8, R2: 16, RM: 24}


def dot_nn(a, b):
    return lax.dot_general(a, b, (((1,), (0,)), ((), ())), preferred_element_type=F32)


def dot_nt(a, b):
    return lax.dot_general(a, b, (((1,), (1,)), ((), ())), preferred_element_type=F32)


def dot_tn(a, b):
    return lax.dot_general(a, b, (((0,), (0,)), ((), ())), preferred_element_type=F32)


def window(head):
    low = HEAD * head // 128 * 128
    high = -(-(HEAD * (head + 1)) // 128) * 128
    return low, high


def head_mask(head):
    low, high = window(head)
    lane = lax.broadcasted_iota(jnp.int32, (1, high - low), 1) + low
    return jnp.where((lane >= HEAD * head) & (lane < HEAD * (head + 1)), 1.0, 0.0).astype(BF16)


def kernel(
    query_shard,
    keyval_shard,
    cross_out_shard,
    qkv_shard,
    time_out_shard,
    latents,
    caption,
    length_ref,
    modulation,
    cotangent,
    out_ref,
    grad_latents,
    grad_mod,
    grad_weight,
    cols_a,
    cols_b,
    qkv_wide,
    pair_rows,
    z_wide_send,
    z_send,
    z_recv,
    z_wide,
    z_rows,
    own,
    keyval_wide,
    latent_rows,
    rows_wide,
    latent_recv,
    att_send,
    att_recv,
    wa,
    wb,
    cross_out,
    time_out,
    keys,
    values,
    queries,
    probs_c,
    acc,
    hidden_rows,
    gm_send,
    gm_recv,
    mix_send,
    mix_recv,
    term_send,
    term_recv,
    normed_ref,
    packed_ref,
    probs_t,
    grad_branch,
    gw_send,
    gw_core,
    gw_half,
    gw_x,
    gw_part,
    gw_y1,
    gw_part1,
    gw_y,
    gw_tile,
    gw_z,
    gw_red,
    gw_all,
    gw_last,
    mod_sum,
    mod_y,
    mod_tile,
    mod_z,
    zs_send,
    zs_recv,
    ring_send,
    a_recv,
    b_recv,
    core_send,
    core_recv,
    local_sem,
    all_send,
    all_recv,
    red_send,
    red_recv,
    core_part_recv,
):
    dp, s = lax.axis_index("dp"), lax.axis_index("seq")
    x, zh, c = dp // 4, (dp // 2) % 2, dp % 2
    y, zl = s // 8, s % 8
    z = zh * 8 + zl
    u = c * 4 + x

    def at(px, py, pz, pc):
        px, py, pz = lax.rem(px + 4, 4), lax.rem(py + 4, 4), lax.rem(pz + 16, 16)
        return (px * 4 + (pz // 8) * 2 + pc, py * 8 + lax.rem(pz, 8))

    def remote(src, dst, send, recv, device):
        return pltpu.make_async_remote_copy(
            src_ref=src, dst_ref=dst, send_sem=send, recv_sem=recv, device_id=device, device_id_type=MESH
        )

    def wait_bytes(ref, sem):
        pltpu.make_async_copy(ref, ref, sem).wait()

    barrier = pltpu.get_barrier_semaphore()

    def greet(i, carry):
        pl.semaphore_signal(barrier, inc=1, device_id=(dp, lax.rem(s + i, SEQ)), device_id_type=MESH)
        return carry

    lax.fori_loop(1, SEQ, greet, 0)
    for i in range(8):
        pl.semaphore_signal(barrier, inc=1, device_id=at(x, y, (1 - zh) * 8 + i, c), device_id_type=MESH)
    for i in range(1, 8):
        peer = lax.rem(x * 2 + c + i, 8)
        pl.semaphore_signal(barrier, inc=1, device_id=at(peer // 2, y, z, peer % 2), device_id_type=MESH)

    cols_a[...] = jnp.zeros_like(cols_a)
    qkv_wide[...] = jnp.zeros_like(qkv_wide)
    z_wide_send[...] = jnp.zeros_like(z_wide_send)
    cols_a[0:36, 0:1152] = keyval_shard[...].astype(F32)
    cols_a[0:36, 1152:1728] = query_shard[...].astype(F32)
    qkv_wide[0:36, 0:1728] = qkv_shard[...].astype(F32)
    turned = pltpu.roll(qkv_wide[...], 64, 1)
    cols_a[:, 1664:1792] += turned[:, 0:128]
    cols_a[:, 1792:3456] = turned[:, 128:1792]
    cols_b[0:18, 0:128] = time_out_shard[:, 1024:1152].astype(F32)
    cols_b[0:18, 128:1280] = cross_out_shard[...].astype(F32)
    cols_b[0:18, 1280:2304] = time_out_shard[:, 0:1024].astype(F32)

    def block_of(first):
        return pl.ds(pl.multiple_of(first * 128, 128), 128)

    z_wide_send[0:36, :] = cols_a[0:36, block_of(u)]
    z_wide_send[36:72, :] = cols_a[0:36, block_of(8 + u)]
    z_wide_send[128:164, :] = cols_a[0:36, block_of(16 + u)]
    z_wide_send[108:126, :] = cols_b[0:18, block_of(10 + u)]
    pair = lax.max(u - 3, 0)
    pair_rows[0:18, :] = cols_b[0:18, block_of(2 * pair)]
    pair_rows[18:36, :] = cols_b[0:18, block_of(2 * pair + 1)]
    z_wide_send[72:108, :] = jnp.where(u < 3, cols_a[0:36, block_of(lax.min(24 + u, 26))], pair_rows[0:36, :])
    z_send[...] = z_wide_send[...].astype(BF16)

    pl.semaphore_wait(barrier, 31 + 8 + 7)

    def along_z(part, first, count, step):
        rows = pl.ds(first, count)
        remote(
            z_send.at[rows], z_recv.at[zl, rows], zs_send.at[part], zs_recv.at[part], at(x, y, z + step, c)
        ).start()

    for part, first, cut, count in ((0, 0, 64, 128), (1, 128, 32, 48)):
        for step in (1, -1, 2, -2, 3, -3):
            along_z(part, first, count, step)
        along_z(part, first, cut, 4)
        along_z(part, first + cut, count - cut, -4)
    z_recv[pl.ds(zl, 1)] = z_send[...].reshape(1, 176, 128)

    shift_row = modulation[0]
    scale_row = 1.0 + modulation[1]
    gate_row = modulation[2]
    grad_branch[...] = (gate_row * cotangent[...].astype(F32)).astype(BF16)
    latent_rows[...] = latents[...].astype(F32).reshape(ROWS, MODEL).astype(BF16)
    keys[...] = jnp.zeros_like(keys)
    values[...] = jnp.zeros_like(values)
    keyval_wide[296:304, :] = jnp.zeros((8, MODEL), F32)
    rows_wide[...] = jnp.zeros_like(rows_wide)
    cross_out[INNER:WIDE, :] = jnp.zeros((WIDE - INNER, MODEL), BF16)
    time_out[INNER:WIDE, :] = jnp.zeros((WIDE - INNER, MODEL), BF16)
    mod_sum[...] = jnp.zeros_like(mod_sum)

    def place(i, j):
        px = lax.rem(x + i * (1 - c) + j * c + 4, 4)
        py = lax.rem(y + i * c + j * (1 - c) + 4, 4)
        return px, py

    def neighbour(i, j):
        px, py = place(i, j)
        return at(px, py, z, c)

    def piece(k, i, j, half=None):
        px, py = place(i, j)
        count = 144 if k == RB else 288
        start, size = 0, count
        if half is not None:
            cut = 80 if k == RB else 144
            start, size = (0, cut) if half == 0 else (cut, count - cut)
        buf = wb if k == RB else wa
        row = pl.multiple_of(py * count + start, 16)
        col = pl.multiple_of((FIRST_BLOCK[k] + 4 * c + px) * 128, 128)
        return buf.at[pl.ds(row, size), pl.ds(col, 128)]

    def own_piece(k):
        return own.at[pl.ds(STAGED[k], 144 if k == RB else 288)]

    def pieces_like(k, count):
        return wa.at[pl.ds(0, 144 if k == RB else 288), pl.ds(0, 128 * count)]

    def halves_like(k, half, count):
        size = (80 if half == 0 else 64) if k == RB else 144
        return wa.at[pl.ds(0, size), pl.ds(0, 128 * count)]

    def core_part(k, core):
        buf = wb if k == RB else wa
        col = pl.multiple_of((FIRST_BLOCK[k] + 4 * core) * 128, 128)
        return buf.at[:, pl.ds(col, 512)]

    def stage1(k):
        pltpu.make_async_copy(own_piece(k), piece(k, 0, 0), local_sem.at[k]).start()
        for side, step in ((0, 1), (1, -1)):
            remote(own_piece(k), piece(k, 0, 0), ring_send.at[k], a_recv.at[k, side], neighbour(step, 0)).start()

    def stage2(k):
        for side, step in ((0, 1), (1, -1)):
            wait_bytes(piece(k, -step, 0), a_recv.at[k, side])
            ref = piece(k, -step, 0, half=side)
            remote(ref, ref, ring_send.at[k], a_recv.at[k, 2 + side], neighbour(step, 0)).start()
        for i in (0, -1, 1):
            for side, step in ((0, 1), (1, -1)):
                src = own_piece(k) if i == 0 else piece(k, i, 0)
                remote(src, piece(k, i, 0), ring_send.at[k], b_recv.at[k, side], neighbour(0, step)).start()

    def stage3(k):
        for side in (0, 1):
            wait_bytes(halves_like(k, side, 1), a_recv.at[k, 2 + side])
        for side, step in ((0, 1), (1, -1)):
            ref = piece(k, 2, 0)
            remote(ref, ref, ring_send.at[k], b_recv.at[k, side], neighbour(0, step)).start()
        pltpu.make_async_copy(own_piece(k), piece(k, 0, 0), local_sem.at[k]).wait()
        to_core(k, [(i, 0) for i in (0, -1, 1, 2)])

    def stage4(k):
        for side, step in ((0, 1), (1, -1)):
            wait_bytes(pieces_like(k, 4), b_recv.at[k, side])
            for i in (0, -1, 1, 2):
                ref = piece(k, i, -step, half=side)
                remote(ref, ref, ring_send.at[k], b_recv.at[k, 2 + side], neighbour(0, step)).start()
        to_core(k, [(i, j) for j in (-1, 1) for i in (0, -1, 1, 2)])

    def to_core(k, places):
        for i, j in places:
            ref = piece(k, i, j)
            remote(ref, ref, core_send.at[k], core_recv.at[k], at(x, y, z, 1 - c)).start()

    def stage5(k):
        for side in (0, 1):
            wait_bytes(halves_like(k, side, 4), b_recv.at[k, 2 + side])
        to_core(k, [(i, 2) for i in (0, -1, 1, 2)])

    def stage6(k):
        wait_bytes(core_part(k, 1 - c), core_recv.at[k])

    def exchange(src, dst, index, first=1, last=SEQ):
        def send(i, carry):
            d = lax.rem(s + i, SEQ)
            remote(src.at[d], dst.at[s], all_send.at[index], all_recv.at[index], (dp, d)).start()
            return carry

        lax.fori_loop(first, last, send, 0)
        if first == 1:
            dst[pl.ds(s, 1)] = src[pl.ds(s, 1)]

    def arrived(dst, index):
        wait_bytes(dst.at[pl.ds(0, 31)], all_recv.at[index])

    def unpack_pairs():
        for slot in range(5):
            col = (27 + slot) * 128
            for half in range(2):
                block = 2 * slot + half
                for part in range(4):
                    rows = slice(288 * part + 144 * half, 288 * part + 144 * half + 144)
                    target = slice(144 * part, 144 * part + 144)
                    if block == 0:
                        time_out[target, 1024:1152] = wa[rows, col : col + 128]
                    else:
                        cross_out[target, (block - 1) * 128 : block * 128] = wa[rows, col : col + 128]

    def put_rows(recv):
        rows_wide[:, 0:INNER] = recv[...].astype(F32).reshape(ROWS, INNER).astype(BF16)

    order = (RB, RM, R0, R1, R2)
    early = (RB, RM, R0, R1)
    late = (R2,)
    wait_bytes(z_recv.at[pl.ds(0, 7), pl.ds(0, 128)], zs_recv.at[0])
    z_wide[:, 0:128, :] = z_recv[:, 0:128, :].astype(F32)

    def spread(k, first):
        base = STAGED[k]
        for j in range(8):
            z_rows[base + 36 * j : base + 36 * j + 36, :] = z_wide[j, first : first + 36, :]
        own[base : base + 288, :] = z_rows[base : base + 288, :].astype(BF16)

    for j in range(8):
        z_rows[576 + 36 * j : 612 + 36 * j, :] = z_wide[j, 72:108, :]
        z_rows[1296 + 18 * j : 1314 + 18 * j, :] = z_wide[j, 72:90, :]
        z_rows[1440 + 18 * j : 1458 + 18 * j, :] = z_wide[j, 90:108, :]
        z_rows[864 + 18 * j : 882 + 18 * j, :] = z_wide[j, 108:126, :]
    own[576:864, :] = jnp.where(u < 3, z_rows[576:864, :], z_rows[1296:1584, :]).astype(BF16)
    own[864:1008, :] = z_rows[864:1008, :].astype(BF16)
    stage1(RB)
    stage1(RM)
    spread(R0, 0)
    stage1(R0)
    spread(R1, 36)
    stage1(R1)
    exchange(latents, latent_recv, 1, 1, 5)
    wait_bytes(z_recv.at[pl.ds(0, 7), pl.ds(128, 48)], zs_recv.at[1])
    z_wide[:, 128:176, :] = z_recv[:, 128:176, :].astype(F32)
    spread(R2, 128)
    sent = 5
    for stage in (stage2, stage3, stage4, stage5):
        for k in early:
            stage(k)
            if sent < SEQ:
                exchange(latents, latent_recv, 1, sent, min(sent + 2, SEQ))
                sent += 2
    for k in late:
        stage1(k)

    stage6(RB)
    stage6(RM)
    unpack_pairs()
    time_out[0:INNER, 0:1024] = wb[...]
    grad_mixed = dot_nt(grad_branch[...], time_out[...])
    gm_send[...] = grad_mixed[:, 0:INNER].reshape(SEQ, 8, INNER).astype(BF16)
    exchange(gm_send, gm_recv, 0)

    stage6(R0)
    stage6(R1)
    keyval_wide[0:300, :] = dot_nn(caption[...], wa[:, 0:1152])
    keys[0:304, 0:INNER] = keyval_wide[:, 0:INNER].astype(BF16)
    turned = pltpu.roll(keyval_wide[:, 512:1152], 576, 1)
    values[0:304, 0:INNER] = turned[:, 0:INNER].astype(BF16)
    for k in late:
        stage2(k)
    queries[...] = dot_nn(latent_rows[...], wa[:, 1152:1792]).astype(BF16)
    for k in late:
        stage3(k)

    slot = lax.broadcasted_iota(jnp.int32, (1, SLOTS), 1)
    bias = jnp.where(slot < length_ref[0], 0.0, NEG)
    acc[...] = jnp.zeros_like(acc)
    for head in range(HEADS):
        low, high = window(head)
        mask = head_mask(head)
        scores = dot_nt(queries[:, low:high], keys[:, low:high] * mask) * HEAD_SCALE + bias
        weight = jnp.exp(scores - jnp.max(scores, axis=1, keepdims=True))
        soft = weight / jnp.sum(weight, axis=1, keepdims=True)
        probs_c[head] = soft
        acc[:, low:high] += dot_nn(soft.astype(BF16), values[:, low:high] * mask)
    attended = acc[...]
    att_send[...] = attended[:, 0:INNER].reshape(SEQ, 8, INNER).astype(BF16)
    exchange(att_send, att_recv, 4)
    for stage in (stage4, stage5):
        for k in late:
            stage(k)
    hidden_rows[...] = (
        latent_rows[...].astype(F32) + dot_nn(attended.astype(BF16), cross_out[...])
    ).astype(BF16)
    stage6(R2)
    arrived(latent_recv, 1)
    arrived(att_recv, 4)

    put_rows(att_recv)
    latent_patch = latent_recv[...].astype(F32).reshape(ROWS, MODEL)
    rows = (latent_patch + dot_nn(rows_wide[...], cross_out[...])).astype(BF16).astype(F32)
    center = rows - jnp.mean(rows, axis=1, keepdims=True)
    inv_std = lax.rsqrt(jnp.mean(center * center, axis=1, keepdims=True) + EPS)
    normed_ref[...] = center * inv_std
    modded = (normed_ref[...] * scale_row + shift_row).astype(BF16)
    packed = dot_nn(modded, wa[:, 1664:3456])
    packed_ref[0] = pltpu.roll(packed[:, 0:640], 576, 1).astype(BF16)
    packed_ref[1] = packed[:, 640:1280].astype(BF16)
    packed_ref[2] = pltpu.roll(packed[:, 1152:1792], 576, 1).astype(BF16)
    same = (
        lax.broadcasted_iota(jnp.int32, (ROWS, ROWS), 0) % 8 == lax.broadcasted_iota(jnp.int32, (ROWS, ROWS), 1) % 8
    )
    acc[...] = jnp.zeros_like(acc)
    for head in range(HEADS):
        low, high = window(head)
        mask = head_mask(head)
        scores = dot_nt(packed_ref[0, :, low:high], packed_ref[1, :, low:high] * mask) * HEAD_SCALE
        scores = jnp.where(same, scores, NEG)
        weight = jnp.exp(scores - jnp.max(scores, axis=1, keepdims=True))
        soft = weight / jnp.sum(weight, axis=1, keepdims=True)
        probs_t[head] = soft
        acc[:, low:high] += dot_nn(soft.astype(BF16), packed_ref[2, :, low:high] * mask)
    mix_send[...] = acc[:, 0:INNER].reshape(SEQ, 8, INNER).astype(BF16)
    exchange(mix_send, mix_recv, 2)

    arrived(gm_recv, 0)
    put_rows(gm_recv)
    parts = [[None] * 5 for _ in range(3)]

    def add_window(store, low, high, value):
        for block in range(low // 128, high // 128):
            piece_value = value[:, block * 128 - low : block * 128 - low + 128]
            store[block] = piece_value if store[block] is None else store[block] + piece_value

    for head in range(HEADS):
        low, high = window(head)
        mask = head_mask(head)
        soft = probs_t[head]
        grad_head = rows_wide[:, low:high] * mask
        grad_soft = dot_nt(grad_head, packed_ref[2, :, low:high])
        delta = jnp.sum(soft * grad_soft, axis=1, keepdims=True)
        grad_scores = (soft * (grad_soft - delta) * HEAD_SCALE).astype(BF16)
        add_window(parts[0], low, high, dot_nn(grad_scores, packed_ref[1, :, low:high] * mask))
        add_window(parts[1], low, high, dot_tn(grad_scores, packed_ref[0, :, low:high] * mask))
        add_window(parts[2], low, high, dot_tn(soft.astype(BF16), grad_head))
    grad_q, grad_k, grad_v = (jnp.concatenate(store, axis=1) for store in parts)
    grad_q = pltpu.roll(grad_q, 64, 1)
    grad_v = pltpu.roll(grad_v, 64, 1)
    grad_packed = jnp.concatenate(
        [grad_q, grad_k[:, 0:512], grad_k[:, 512:640] + grad_v[:, 0:128], grad_v[:, 128:640]], axis=1
    ).astype(BF16)
    grad_modded = dot_nt(grad_packed, wa[:, 1664:3456])
    mod_sum[0:1, 0:MODEL] = jnp.sum(grad_modded, axis=0, keepdims=True)
    mod_sum[1:2, 0:MODEL] = jnp.sum(grad_modded * normed_ref[...], axis=0, keepdims=True)
    grad_norm = grad_modded * scale_row
    first_mean = jnp.mean(grad_norm, axis=1, keepdims=True)
    second_mean = jnp.mean(grad_norm * normed_ref[...], axis=1, keepdims=True)
    term = inv_std * (grad_norm - first_mean - normed_ref[...] * second_mean)
    term_send[...] = term.reshape(SEQ, 8, MODEL).astype(BF16)
    arrived(mix_recv, 2)

    def send_term(first, last):
        exchange(term_send, term_recv, 3, first, last)


    put_rows(mix_recv)
    mixed = rows_wide[...]
    partial = dot_tn(mixed, grad_branch[...])
    gw_send[...] = partial[0:INNER, :].reshape(72, 8, MODEL).astype(BF16)
    for i in (2, 1, 3, 0):
        part = lax.rem(x + i, 4)
        remote(
            gw_send.at[pl.ds(36 * (1 - c) + 9 * part, 9)],
            gw_core.at[pl.ds(9 * part, 9)],
            red_send.at[0],
            core_part_recv.at[part],
            at(x, y, z, 1 - c),
        ).start()
    send_term(1, 8)
    branch = dot_nn(mixed, time_out[...])
    out_ref[...] = (hidden_rows[...].astype(F32) + gate_row * branch).astype(BF16)
    mod_sum[2:3, 0:MODEL] = jnp.sum(cotangent[...].astype(F32) * branch, axis=0, keepdims=True)
    for i in range(1, 4):
        remote(mod_sum, mod_y.at[i - 1], red_send.at[6], red_recv.at[6], at(x, y + i, z, c)).start()

    for i in (2, 1, 3, 0):
        part = lax.rem(x + i, 4)
        rows9 = pl.ds(9 * part, 9)
        wait_bytes(gw_core.at[rows9], core_part_recv.at[part])
        gw_half[rows9] = (
            gw_send[pl.ds(36 * c + 9 * part, 9)].astype(F32) + gw_core[rows9].astype(F32)
        ).astype(BF16)
        if i:

            @pl.when(c == 0)
            def _():
                remote(
                    gw_half.at[rows9], gw_x.at[i - 1], red_send.at[1], red_recv.at[1], at(part, y, z, c)
                ).start()

    own_cols = pl.ds(pl.multiple_of(256 * y, 128), 384)
    own_rows = pl.ds(9 * x, 9)

    def total_of(mine, others):
        total = mine.astype(F32)
        for i in range(3):
            total = total + others[i].astype(F32)
        return total.astype(BF16)

    def to_y(source, target, send, recv):
        for i in (2, 1, 3):
            to = lax.rem(y + i, 4)
            cols = pl.ds(pl.multiple_of(256 * to, 128), 384)
            remote(source.at[:, :, cols], target.at[i - 1], send, recv, at(x, to, z, c)).start()

    @pl.when(c == 1)
    def _():
        to_y(gw_half, gw_y1, red_send.at[1], red_recv.at[1])

    send_term(8, 14)

    wait_bytes(mod_y, red_recv.at[6])
    mod_tile[...] = mod_sum[...] + mod_y[0] + mod_y[1] + mod_y[2]
    for i in range(1, 8):
        to = lax.rem(zl + i, 8)
        block = (36 * (8 * y + to)) // 128
        col = pl.multiple_of(block * 128, 128)
        remote(
            mod_tile.at[:, pl.ds(col, 256)], mod_z.at[i - 1], red_send.at[7], red_recv.at[7], (dp, 8 * y + to)
        ).start()

    @pl.when(c == 0)
    def _():
        wait_bytes(gw_x, red_recv.at[1])
        gw_part[...] = total_of(gw_half[own_rows], gw_x)
        to_y(gw_part, gw_y, red_send.at[2], red_recv.at[2])
        send_term(14, 20)
        wait_bytes(gw_y, red_recv.at[2])
        gw_tile[...] = total_of(gw_part[:, :, own_cols], gw_y)

    @pl.when(c == 1)
    def _():
        wait_bytes(gw_y1, red_recv.at[1])
        gw_part1[...] = total_of(gw_half[:, :, own_cols], gw_y1)
        for i in (2, 1, 3):
            to = lax.rem(x + i, 4)
            remote(
                gw_part1.at[pl.ds(9 * to, 9)], gw_y.at[i - 1], red_send.at[2], red_recv.at[2], at(to, y, z, c)
            ).start()
        send_term(14, 20)
        wait_bytes(gw_y, red_recv.at[2])
        gw_tile[...] = total_of(gw_part1[own_rows], gw_y)

    for group in range(9):

        @pl.when(z != group)
        def _():
            remote(
                gw_tile.at[group], gw_z.at[z], red_send.at[3], red_recv.at[3], at(x, y, jnp.int32(group), c)
            ).start()

    send_term(20, 26)
    @pl.when(z < 9)
    def _():
        wait_bytes(gw_z.at[pl.ds(0, 15)], red_recv.at[3])
        gw_z[pl.ds(z, 1)] = gw_tile[pl.ds(z, 1)]
        total = jnp.sum(gw_z[...].astype(F32), axis=0)
        for place_z in range(8):
            turned = pltpu.roll(total, 384 - (32 * y + 36 * place_z), 1)
            gw_red[place_z] = turned[:, 0:128].astype(BF16)
        gw_all[pl.ds(z, 1)] = gw_red[pl.ds(zl, 1)]

        def send(i, carry):
            remote(
                gw_red.at[lax.rem(zl + i, 8)], gw_all.at[z], red_send.at[4], red_recv.at[4], at(x, y, z + i, c)
            ).start()
            return carry

        lax.fori_loop(1, 16, send, 0)

    send_term(26, SEQ)
    arrived(term_recv, 3)
    grad_hidden = (
        cotangent[...].astype(F32) + term_recv[...].astype(F32).reshape(ROWS, MODEL)
    ).astype(BF16)
    grad_attended = dot_nt(grad_hidden, cross_out[...]).astype(BF16)
    acc[...] = jnp.zeros_like(acc)

    def back(head):
        low, high = window(head)
        mask = head_mask(head)
        soft = probs_c[head]
        grad_soft = dot_nt(grad_attended[:, low:high], values[:, low:high] * mask)
        delta = jnp.sum(soft * grad_soft, axis=1, keepdims=True)
        grad_scores = (soft * (grad_soft - delta) * HEAD_SCALE).astype(BF16)
        acc[:, low:high] += dot_nn(grad_scores, keys[:, low:high] * mask)

    for head in range(4):
        back(head)

    @pl.when(z < 9)
    def _():
        wait_bytes(gw_all.at[pl.ds(0, 8)], red_recv.at[4])

    @pl.when(z >= 9)
    def _():
        wait_bytes(gw_all, red_recv.at[4])

    gw_last[pl.ds(u, 1)] = gw_all[...].reshape(1, 9, 8, 128)
    for i in range(1, 8):
        peer = lax.rem(x * 2 + c + i, 8)
        remote(
            gw_all, gw_last.at[u], red_send.at[5], red_recv.at[5], at(peer // 2, y, z, peer % 2)
        ).start()

    for head in range(4, HEADS):
        back(head)
    grad_latents[...] = (
        grad_hidden.astype(F32) + dot_nt(acc[...].astype(BF16), wa[:, 1152:1792])
    ).astype(BF16)

    wait_bytes(mod_z, red_recv.at[7])
    block = (36 * s) // 128
    mod_total = mod_tile[:, pl.ds(pl.multiple_of(block * 128, 128), 256)]
    for i in range(7):
        mod_total = mod_total + mod_z[i]
    mod_total = pltpu.roll(mod_total, lax.rem(256 - (36 * s - 128 * block), 256), 1)
    for i in range(3):
        grad_mod[i] = mod_total[i : i + 1, 0:36] * (SEQ * ROWS) ** (-0.5)

    wait_bytes(gw_last.at[pl.ds(0, 7)], red_recv.at[5])
    total = jnp.transpose(gw_last[...].astype(F32).reshape(INNER, 128))
    grad_weight[...] = total[0:36, :] * (SEQ * ROWS * 16) ** (-0.5)

    wait_bytes(z_recv.at[pl.ds(0, 7), pl.ds(0, 128)], zs_send.at[0])
    wait_bytes(z_recv.at[pl.ds(0, 7), pl.ds(128, 48)], zs_send.at[1])
    for k in order:
        if k == RB:
            wait_bytes(wa.at[pl.ds(0, 144), pl.ds(0, 128 * 15)], ring_send.at[k])
        else:
            wait_bytes(pieces_like(k, 15), ring_send.at[k])
        wait_bytes(core_part(k, c), core_send.at[k])
    for index, ref in ((0, gm_recv), (1, latent_recv), (2, mix_recv), (3, term_recv), (4, att_recv)):
        wait_bytes(ref.at[pl.ds(0, 31)], all_send.at[index])
    wait_bytes(gw_core, red_send.at[0])
    wait_bytes(gw_y, red_send.at[2])

    @pl.when(c == 0)
    def _():
        wait_bytes(gw_x, red_send.at[1])

    @pl.when(c == 1)
    def _():
        wait_bytes(gw_y1, red_send.at[1])


    @pl.when(z < 9)
    def _():
        wait_bytes(gw_z.at[pl.ds(0, 8)], red_send.at[3])
        wait_bytes(gw_z.at[pl.ds(0, 15), :, pl.ds(0, 128)], red_send.at[4])

    @pl.when(z >= 9)
    def _():
        wait_bytes(gw_z.at[pl.ds(0, 9)], red_send.at[3])

    wait_bytes(gw_last.at[pl.ds(0, 7)], red_send.at[5])
    wait_bytes(mod_y, red_send.at[6])
    wait_bytes(mod_z, red_send.at[7])


def body(
    latents,
    caption,
    caption_len,
    modulation,
    cross_query,
    cross_keyval,
    cross_output,
    time_qkv,
    time_output,
    cotangent,
):
    vmem = pl.BlockSpec(memory_space=pltpu.VMEM)
    sems = pltpu.SemaphoreType.DMA
    out, grad_in, grad_mod, grad_w = pl.pallas_call(
        kernel,
        out_shape=(
            jax.ShapeDtypeStruct((ROWS, MODEL), BF16),
            jax.ShapeDtypeStruct((ROWS, MODEL), BF16),
            jax.ShapeDtypeStruct((3, 1, 36), F32),
            jax.ShapeDtypeStruct((36, INNER), F32),
        ),
        in_specs=[vmem] * 7 + [pl.BlockSpec(memory_space=pltpu.SMEM)] + [vmem] * 2,
        out_specs=(vmem,) * 4,
        scratch_shapes=[
            pltpu.VMEM((40, 3456), F32),
            pltpu.VMEM((24, 2304), F32),
            pltpu.VMEM((40, 1792), F32),
            pltpu.VMEM((40, 128), F32),
            pltpu.VMEM((176, 128), F32),
            pltpu.VMEM((176, 128), BF16),
            pltpu.VMEM((8, 176, 128), BF16),
            pltpu.VMEM((8, 176, 128), F32),
            pltpu.VMEM((1584, 128), F32),
            pltpu.VMEM((1296, 128), BF16),
            pltpu.VMEM((304, MODEL), F32),
            pltpu.VMEM((ROWS, MODEL), BF16),
            pltpu.VMEM((ROWS, WIDE), BF16),
            pltpu.VMEM((SEQ, 8, MODEL), BF16),
            pltpu.VMEM((SEQ, 8, INNER), BF16),
            pltpu.VMEM((SEQ, 8, INNER), BF16),
            pltpu.VMEM((MODEL, 4096), BF16),
            pltpu.VMEM((INNER, 1024), BF16),
            pltpu.VMEM((WIDE, MODEL), BF16),
            pltpu.VMEM((WIDE, MODEL), BF16),
            pltpu.VMEM((SLOTS, WIDE), BF16),
            pltpu.VMEM((SLOTS, WIDE), BF16),
            pltpu.VMEM((ROWS, WIDE), BF16),
            pltpu.VMEM((HEADS, ROWS, SLOTS), F32),
            pltpu.VMEM((ROWS, WIDE), F32),
            pltpu.VMEM((ROWS, MODEL), BF16),
            pltpu.VMEM((SEQ, 8, INNER), BF16),
            pltpu.VMEM((SEQ, 8, INNER), BF16),
            pltpu.VMEM((SEQ, 8, INNER), BF16),
            pltpu.VMEM((SEQ, 8, INNER), BF16),
            pltpu.VMEM((SEQ, 8, MODEL), BF16),
            pltpu.VMEM((SEQ, 8, MODEL), BF16),
            pltpu.VMEM((ROWS, MODEL), F32),
            pltpu.VMEM((3, ROWS, WIDE), BF16),
            pltpu.VMEM((HEADS, ROWS, ROWS), F32),
            pltpu.VMEM((ROWS, MODEL), BF16),
            pltpu.VMEM((72, 8, MODEL), BF16),
            pltpu.VMEM((36, 8, MODEL), BF16),
            pltpu.VMEM((36, 8, MODEL), BF16),
            pltpu.VMEM((3, 9, 8, MODEL), BF16),
            pltpu.VMEM((9, 8, MODEL), BF16),
            pltpu.VMEM((3, 36, 8, 384), BF16),
            pltpu.VMEM((36, 8, 384), BF16),
            pltpu.VMEM((3, 9, 8, 384), BF16),
            pltpu.VMEM((9, 8, 384), BF16),
            pltpu.VMEM((16, 8, 384), BF16),
            pltpu.VMEM((8, 8, 128), BF16),
            pltpu.VMEM((9, 8, 128), BF16),
            pltpu.VMEM((8, 9, 8, 128), BF16),
            pltpu.VMEM((8, 1280), F32),
            pltpu.VMEM((3, 8, 1280), F32),
            pltpu.VMEM((8, 1280), F32),
            pltpu.VMEM((7, 8, 256), F32),
            sems((2,)),
            sems((2,)),
            sems((5,)),
            sems((5, 4)),
            sems((5, 4)),
            sems((5,)),
            sems((5,)),
            sems((5,)),
            sems((5,)),
            sems((5,)),
            sems((8,)),
            sems((8,)),
            sems((4,)),
        ],
        compiler_params=pltpu.CompilerParams(
            collective_id=0, has_side_effects=True, vmem_limit_bytes=60 * 2**20
        ),
    )(
        cross_query,
        cross_keyval,
        cross_output,
        time_qkv,
        time_output,
        latents.reshape(SEQ, 8, MODEL),
        caption[0],
        caption_len,
        jnp.swapaxes(modulation, 0, 1),
        cotangent.reshape(ROWS, MODEL),
    )
    return (
        out.reshape(latents.shape),
        grad_in.reshape(latents.shape),
        jnp.swapaxes(grad_mod, 0, 1),
        jnp.swapaxes(grad_w, 0, 1),
    )


def solution(mesh):
    placed = (
        P("dp", "seq", None, None),
        P("dp", None, None),
        P("dp"),
        P("dp", None, None),
        P("seq", None),
        P("seq", None),
        P("seq", None),
        P("seq", None),
        P("seq", None),
        P("dp", "seq", None, None),
    )
    return jax.shard_map(
        body,
        mesh=mesh,
        in_specs=placed,
        out_specs=(
            P("dp", "seq", None, None),
            P("dp", "seq", None, None),
            P("dp", None, "seq"),
            P(None, "seq"),
        ),
        check_vma=False,
    )
```

```python
import jax
import jax.numpy as jnp
from jax import lax
from jax.experimental import pallas as pl
from jax.experimental.pallas import tpu as pltpu
from jax.sharding import PartitionSpec as P

MESH = pl.DeviceIdType.MESH
F32 = jnp.float32
BF16 = jnp.bfloat16
HEADS = 8
HEAD = 72
INNER = HEADS * HEAD
WIDE = 640
MODEL = 1152
ROWS = 256
SLOTS = 384
SEQ = 32
EPS = 1e-6
NEG = -1e30
HEAD_SCALE = HEAD ** (-0.5)
RB, R0, R1, RM, R2 = range(5)
STAGED = {R0: 0, R1: 288, RM: 576, RB: 864, R2: 1008}
FIRST_BLOCK = {RB: 0, R0: 0, R1: 8, R2: 16, RM: 24}


def dot_nn(a, b):
    return lax.dot_general(a, b, (((1,), (0,)), ((), ())), preferred_element_type=F32)


def dot_nt(a, b):
    return lax.dot_general(a, b, (((1,), (1,)), ((), ())), preferred_element_type=F32)


def dot_tn(a, b):
    return lax.dot_general(a, b, (((0,), (0,)), ((), ())), preferred_element_type=F32)


def window(head):
    low = HEAD * head // 128 * 128
    high = -(-(HEAD * (head + 1)) // 128) * 128
    return low, high


def head_mask(head):
    low, high = window(head)
    lane = lax.broadcasted_iota(jnp.int32, (1, high - low), 1) + low
    return jnp.where((lane >= HEAD * head) & (lane < HEAD * (head + 1)), 1.0, 0.0).astype(BF16)


def kernel(
    query_shard,
    keyval_shard,
    cross_out_shard,
    qkv_shard,
    time_out_shard,
    latents,
    caption,
    length_ref,
    modulation,
    cotangent,
    out_ref,
    grad_latents,
    grad_mod,
    grad_weight,
    cols_a,
    cols_b,
    qkv_wide,
    pair_rows,
    z_wide_send,
    z_send,
    z_recv,
    z_wide,
    z_rows,
    own,
    keyval_wide,
    latent_rows,
    rows_wide,
    latent_recv,
    att_send,
    att_recv,
    wa,
    wb,
    cross_out,
    time_out,
    keys,
    values,
    queries,
    probs_c,
    acc,
    hidden_rows,
    gm_send,
    gm_recv,
    mix_send,
    mix_recv,
    term_send,
    term_recv,
    normed_ref,
    packed_ref,
    probs_t,
    grad_branch,
    gw_send,
    gw_core,
    gw_half,
    gw_x,
    gw_part,
    gw_y1,
    gw_part1,
    gw_y,
    gw_tile,
    gw_z,
    gw_red,
    gw_all,
    gw_last,
    mod_sum,
    mod_y,
    mod_tile,
    mod_z,
    zs_send,
    zs_recv,
    ring_send,
    a_recv,
    b_recv,
    core_send,
    core_recv,
    local_sem,
    all_send,
    all_recv,
    red_send,
    red_recv,
    core_part_recv,
):
    dp, s = lax.axis_index("dp"), lax.axis_index("seq")
    x, zh, c = dp // 4, (dp // 2) % 2, dp % 2
    y, zl = s // 8, s % 8
    z = zh * 8 + zl
    u = c * 4 + x

    def at(px, py, pz, pc):
        px, py, pz = lax.rem(px + 4, 4), lax.rem(py + 4, 4), lax.rem(pz + 16, 16)
        return (px * 4 + (pz // 8) * 2 + pc, py * 8 + lax.rem(pz, 8))

    def remote(src, dst, send, recv, device):
        return pltpu.make_async_remote_copy(
            src_ref=src, dst_ref=dst, send_sem=send, recv_sem=recv, device_id=device, device_id_type=MESH
        )

    def wait_bytes(ref, sem):
        pltpu.make_async_copy(ref, ref, sem).wait()

    barrier = pltpu.get_barrier_semaphore()

    def greet(i, carry):
        pl.semaphore_signal(barrier, inc=1, device_id=(dp, lax.rem(s + i, SEQ)), device_id_type=MESH)
        return carry

    lax.fori_loop(1, SEQ, greet, 0)
    for i in range(8):
        pl.semaphore_signal(barrier, inc=1, device_id=at(x, y, (1 - zh) * 8 + i, c), device_id_type=MESH)
    for i in range(1, 8):
        peer = lax.rem(x * 2 + c + i, 8)
        pl.semaphore_signal(barrier, inc=1, device_id=at(peer // 2, y, z, peer % 2), device_id_type=MESH)

    cols_a[...] = jnp.zeros_like(cols_a)
    qkv_wide[...] = jnp.zeros_like(qkv_wide)
    z_wide_send[...] = jnp.zeros_like(z_wide_send)
    cols_a[0:36, 0:1152] = keyval_shard[...].astype(F32)
    cols_a[0:36, 1152:1728] = query_shard[...].astype(F32)
    qkv_wide[0:36, 0:1728] = qkv_shard[...].astype(F32)
    turned = pltpu.roll(qkv_wide[...], 64, 1)
    cols_a[:, 1664:1792] += turned[:, 0:128]
    cols_a[:, 1792:3456] = turned[:, 128:1792]
    cols_b[0:18, 0:128] = time_out_shard[:, 1024:1152].astype(F32)
    cols_b[0:18, 128:1280] = cross_out_shard[...].astype(F32)
    cols_b[0:18, 1280:2304] = time_out_shard[:, 0:1024].astype(F32)

    def block_of(first):
        return pl.ds(pl.multiple_of(first * 128, 128), 128)

    z_wide_send[0:36, :] = cols_a[0:36, block_of(u)]
    z_wide_send[36:72, :] = cols_a[0:36, block_of(8 + u)]
    z_wide_send[128:164, :] = cols_a[0:36, block_of(16 + u)]
    z_wide_send[108:126, :] = cols_b[0:18, block_of(10 + u)]
    pair = lax.max(u - 3, 0)
    pair_rows[0:18, :] = cols_b[0:18, block_of(2 * pair)]
    pair_rows[18:36, :] = cols_b[0:18, block_of(2 * pair + 1)]
    z_wide_send[72:108, :] = jnp.where(u < 3, cols_a[0:36, block_of(lax.min(24 + u, 26))], pair_rows[0:36, :])
    z_send[...] = z_wide_send[...].astype(BF16)

    pl.semaphore_wait(barrier, 31 + 8 + 7)

    def along_z(part, first, count, step):
        rows = pl.ds(first, count)
        remote(
            z_send.at[rows], z_recv.at[zl, rows], zs_send.at[part], zs_recv.at[part], at(x, y, z + step, c)
        ).start()

    for part, first, cut, count in ((0, 0, 64, 128), (1, 128, 32, 48)):
        for step in (1, -1, 2, -2, 3, -3):
            along_z(part, first, count, step)
        along_z(part, first, cut, 4)
        along_z(part, first + cut, count - cut, -4)
    z_recv[pl.ds(zl, 1)] = z_send[...].reshape(1, 176, 128)

    shift_row = modulation[0]
    scale_row = 1.0 + modulation[1]
    gate_row = modulation[2]
    grad_branch[...] = (gate_row * cotangent[...].astype(F32)).astype(BF16)
    latent_rows[...] = latents[...].astype(F32).reshape(ROWS, MODEL).astype(BF16)
    keys[...] = jnp.zeros_like(keys)
    values[...] = jnp.zeros_like(values)
    keyval_wide[296:304, :] = jnp.zeros((8, MODEL), F32)
    rows_wide[...] = jnp.zeros_like(rows_wide)
    cross_out[INNER:WIDE, :] = jnp.zeros((WIDE - INNER, MODEL), BF16)
    time_out[INNER:WIDE, :] = jnp.zeros((WIDE - INNER, MODEL), BF16)
    mod_sum[...] = jnp.zeros_like(mod_sum)

    def place(i, j):
        px = lax.rem(x + i * (1 - c) + j * c + 4, 4)
        py = lax.rem(y + i * c + j * (1 - c) + 4, 4)
        return px, py

    def neighbour(i, j):
        px, py = place(i, j)
        return at(px, py, z, c)

    def piece(k, i, j, half=None):
        px, py = place(i, j)
        count = 144 if k == RB else 288
        start, size = 0, count
        if half is not None:
            cut = 80 if k == RB else 144
            start, size = (0, cut) if half == 0 else (cut, count - cut)
        buf = wb if k == RB else wa
        row = pl.multiple_of(py * count + start, 16)
        col = pl.multiple_of((FIRST_BLOCK[k] + 4 * c + px) * 128, 128)
        return buf.at[pl.ds(row, size), pl.ds(col, 128)]

    def own_piece(k):
        return own.at[pl.ds(STAGED[k], 144 if k == RB else 288)]

    def pieces_like(k, count):
        return wa.at[pl.ds(0, 144 if k == RB else 288), pl.ds(0, 128 * count)]

    def halves_like(k, half, count):
        size = (80 if half == 0 else 64) if k == RB else 144
        return wa.at[pl.ds(0, size), pl.ds(0, 128 * count)]

    def core_part(k, core):
        buf = wb if k == RB else wa
        col = pl.multiple_of((FIRST_BLOCK[k] + 4 * core) * 128, 128)
        return buf.at[:, pl.ds(col, 512)]

    def stage1(k):
        pltpu.make_async_copy(own_piece(k), piece(k, 0, 0), local_sem.at[k]).start()
        for side, step in ((0, 1), (1, -1)):
            remote(own_piece(k), piece(k, 0, 0), ring_send.at[k], a_recv.at[k, side], neighbour(step, 0)).start()

    def stage2(k):
        for side, step in ((0, 1), (1, -1)):
            wait_bytes(piece(k, -step, 0), a_recv.at[k, side])
            ref = piece(k, -step, 0, half=side)
            remote(ref, ref, ring_send.at[k], a_recv.at[k, 2 + side], neighbour(step, 0)).start()
        for i in (0, -1, 1):
            for side, step in ((0, 1), (1, -1)):
                src = own_piece(k) if i == 0 else piece(k, i, 0)
                remote(src, piece(k, i, 0), ring_send.at[k], b_recv.at[k, side], neighbour(0, step)).start()

    def stage3(k):
        for side in (0, 1):
            wait_bytes(halves_like(k, side, 1), a_recv.at[k, 2 + side])
        for side, step in ((0, 1), (1, -1)):
            ref = piece(k, 2, 0)
            remote(ref, ref, ring_send.at[k], b_recv.at[k, side], neighbour(0, step)).start()
        pltpu.make_async_copy(own_piece(k), piece(k, 0, 0), local_sem.at[k]).wait()
        to_core(k, [(i, 0) for i in (0, -1, 1, 2)])

    def stage4(k):
        for side, step in ((0, 1), (1, -1)):
            wait_bytes(pieces_like(k, 4), b_recv.at[k, side])
            for i in (0, -1, 1, 2):
                ref = piece(k, i, -step, half=side)
                remote(ref, ref, ring_send.at[k], b_recv.at[k, 2 + side], neighbour(0, step)).start()
        to_core(k, [(i, j) for j in (-1, 1) for i in (0, -1, 1, 2)])

    def to_core(k, places):
        for i, j in places:
            ref = piece(k, i, j)
            remote(ref, ref, core_send.at[k], core_recv.at[k], at(x, y, z, 1 - c)).start()

    def stage5(k):
        for side in (0, 1):
            wait_bytes(halves_like(k, side, 4), b_recv.at[k, 2 + side])
        to_core(k, [(i, 2) for i in (0, -1, 1, 2)])

    def stage6(k):
        wait_bytes(core_part(k, 1 - c), core_recv.at[k])

    def exchange(src, dst, index, first=1, last=SEQ):
        def send(i, carry):
            d = lax.rem(s + i, SEQ)
            remote(src.at[d], dst.at[s], all_send.at[index], all_recv.at[index], (dp, d)).start()
            return carry

        lax.fori_loop(first, last, send, 0)
        if first == 1:
            dst[pl.ds(s, 1)] = src[pl.ds(s, 1)]

    def arrived(dst, index):
        wait_bytes(dst.at[pl.ds(0, 31)], all_recv.at[index])

    def unpack_pairs():
        for slot in range(5):
            col = (27 + slot) * 128
            for half in range(2):
                block = 2 * slot + half
                for part in range(4):
                    rows = slice(288 * part + 144 * half, 288 * part + 144 * half + 144)
                    target = slice(144 * part, 144 * part + 144)
                    if block == 0:
                        time_out[target, 1024:1152] = wa[rows, col : col + 128]
                    else:
                        cross_out[target, (block - 1) * 128 : block * 128] = wa[rows, col : col + 128]

    def put_rows(recv):
        rows_wide[:, 0:INNER] = recv[...].astype(F32).reshape(ROWS, INNER).astype(BF16)

    order = (RB, RM, R0, R1, R2)
    early = (RB, RM, R0, R1)
    late = (R2,)
    wait_bytes(z_recv.at[pl.ds(0, 7), pl.ds(0, 128)], zs_recv.at[0])
    z_wide[:, 0:128, :] = z_recv[:, 0:128, :].astype(F32)

    def spread(k, first):
        base = STAGED[k]
        for j in range(8):
            z_rows[base + 36 * j : base + 36 * j + 36, :] = z_wide[j, first : first + 36, :]
        own[base : base + 288, :] = z_rows[base : base + 288, :].astype(BF16)

    for j in range(8):
        z_rows[576 + 36 * j : 612 + 36 * j, :] = z_wide[j, 72:108, :]
        z_rows[1296 + 18 * j : 1314 + 18 * j, :] = z_wide[j, 72:90, :]
        z_rows[1440 + 18 * j : 1458 + 18 * j, :] = z_wide[j, 90:108, :]
        z_rows[864 + 18 * j : 882 + 18 * j, :] = z_wide[j, 108:126, :]
    own[576:864, :] = jnp.where(u < 3, z_rows[576:864, :], z_rows[1296:1584, :]).astype(BF16)
    own[864:1008, :] = z_rows[864:1008, :].astype(BF16)
    stage1(RB)
    stage1(RM)
    spread(R0, 0)
    stage1(R0)
    spread(R1, 36)
    stage1(R1)
    exchange(latents, latent_recv, 1, 1, 5)
    wait_bytes(z_recv.at[pl.ds(0, 7), pl.ds(128, 48)], zs_recv.at[1])
    z_wide[:, 128:176, :] = z_recv[:, 128:176, :].astype(F32)
    spread(R2, 128)
    sent = 5
    for stage in (stage2, stage3, stage4, stage5):
        for k in early:
            stage(k)
            if sent < SEQ:
                exchange(latents, latent_recv, 1, sent, min(sent + 2, SEQ))
                sent += 2
    for k in late:
        stage1(k)

    stage6(RB)
    stage6(RM)
    unpack_pairs()
    time_out[0:INNER, 0:1024] = wb[...]
    grad_mixed = dot_nt(grad_branch[...], time_out[...])
    gm_send[...] = grad_mixed[:, 0:INNER].reshape(SEQ, 8, INNER).astype(BF16)
    exchange(gm_send, gm_recv, 0)

    stage6(R0)
    stage6(R1)
    keyval_wide[0:300, :] = dot_nn(caption[...], wa[:, 0:1152])
    keys[0:304, 0:INNER] = keyval_wide[:, 0:INNER].astype(BF16)
    turned = pltpu.roll(keyval_wide[:, 512:1152], 576, 1)
    values[0:304, 0:INNER] = turned[:, 0:INNER].astype(BF16)
    for k in late:
        stage2(k)
    queries[...] = dot_nn(latent_rows[...], wa[:, 1152:1792]).astype(BF16)
    for k in late:
        stage3(k)

    slot = lax.broadcasted_iota(jnp.int32, (1, SLOTS), 1)
    bias = jnp.where(slot < length_ref[0], 0.0, NEG)
    acc[...] = jnp.zeros_like(acc)
    for head in range(HEADS):
        low, high = window(head)
        mask = head_mask(head)
        scores = dot_nt(queries[:, low:high], keys[:, low:high] * mask) * HEAD_SCALE + bias
        weight = jnp.exp(scores - jnp.max(scores, axis=1, keepdims=True))
        soft = weight / jnp.sum(weight, axis=1, keepdims=True)
        probs_c[head] = soft
        acc[:, low:high] += dot_nn(soft.astype(BF16), values[:, low:high] * mask)
    attended = acc[...]
    att_send[...] = attended[:, 0:INNER].reshape(SEQ, 8, INNER).astype(BF16)
    exchange(att_send, att_recv, 4)
    for stage in (stage4, stage5):
        for k in late:
            stage(k)
    hidden_rows[...] = (
        latent_rows[...].astype(F32) + dot_nn(attended.astype(BF16), cross_out[...])
    ).astype(BF16)
    stage6(R2)
    arrived(latent_recv, 1)
    arrived(att_recv, 4)

    put_rows(att_recv)
    latent_patch = latent_recv[...].astype(F32).reshape(ROWS, MODEL)
    rows = (latent_patch + dot_nn(rows_wide[...], cross_out[...])).astype(BF16).astype(F32)
    center = rows - jnp.mean(rows, axis=1, keepdims=True)
    inv_std = lax.rsqrt(jnp.mean(center * center, axis=1, keepdims=True) + EPS)
    normed_ref[...] = center * inv_std
    modded = (normed_ref[...] * scale_row + shift_row).astype(BF16)
    packed = dot_nn(modded, wa[:, 1664:3456])
    packed_ref[0] = pltpu.roll(packed[:, 0:640], 576, 1).astype(BF16)
    packed_ref[1] = packed[:, 640:1280].astype(BF16)
    packed_ref[2] = pltpu.roll(packed[:, 1152:1792], 576, 1).astype(BF16)
    same = (
        lax.broadcasted_iota(jnp.int32, (ROWS, ROWS), 0) % 8 == lax.broadcasted_iota(jnp.int32, (ROWS, ROWS), 1) % 8
    )
    acc[...] = jnp.zeros_like(acc)
    for head in range(HEADS):
        low, high = window(head)
        mask = head_mask(head)
        scores = dot_nt(packed_ref[0, :, low:high], packed_ref[1, :, low:high] * mask) * HEAD_SCALE
        scores = jnp.where(same, scores, NEG)
        weight = jnp.exp(scores - jnp.max(scores, axis=1, keepdims=True))
        soft = weight / jnp.sum(weight, axis=1, keepdims=True)
        probs_t[head] = soft
        acc[:, low:high] += dot_nn(soft.astype(BF16), packed_ref[2, :, low:high] * mask)
    mix_send[...] = acc[:, 0:INNER].reshape(SEQ, 8, INNER).astype(BF16)
    exchange(mix_send, mix_recv, 2)

    arrived(gm_recv, 0)
    put_rows(gm_recv)
    parts = [[None] * 5 for _ in range(3)]

    def add_window(store, low, high, value):
        for block in range(low // 128, high // 128):
            piece_value = value[:, block * 128 - low : block * 128 - low + 128]
            store[block] = piece_value if store[block] is None else store[block] + piece_value

    for head in range(HEADS):
        low, high = window(head)
        mask = head_mask(head)
        soft = probs_t[head]
        grad_head = rows_wide[:, low:high] * mask
        grad_soft = dot_nt(grad_head, packed_ref[2, :, low:high])
        delta = jnp.sum(soft * grad_soft, axis=1, keepdims=True)
        grad_scores = (soft * (grad_soft - delta) * HEAD_SCALE).astype(BF16)
        add_window(parts[0], low, high, dot_nn(grad_scores, packed_ref[1, :, low:high] * mask))
        add_window(parts[1], low, high, dot_tn(grad_scores, packed_ref[0, :, low:high] * mask))
        add_window(parts[2], low, high, dot_tn(soft.astype(BF16), grad_head))
    grad_q, grad_k, grad_v = (jnp.concatenate(store, axis=1) for store in parts)
    grad_q = pltpu.roll(grad_q, 64, 1)
    grad_v = pltpu.roll(grad_v, 64, 1)
    grad_packed = jnp.concatenate(
        [grad_q, grad_k[:, 0:512], grad_k[:, 512:640] + grad_v[:, 0:128], grad_v[:, 128:640]], axis=1
    ).astype(BF16)
    grad_modded = dot_nt(grad_packed, wa[:, 1664:3456])
    mod_sum[0:1, 0:MODEL] = jnp.sum(grad_modded, axis=0, keepdims=True)
    mod_sum[1:2, 0:MODEL] = jnp.sum(grad_modded * normed_ref[...], axis=0, keepdims=True)
    grad_norm = grad_modded * scale_row
    first_mean = jnp.mean(grad_norm, axis=1, keepdims=True)
    second_mean = jnp.mean(grad_norm * normed_ref[...], axis=1, keepdims=True)
    term = inv_std * (grad_norm - first_mean - normed_ref[...] * second_mean)
    term_send[...] = term.reshape(SEQ, 8, MODEL).astype(BF16)

    def send_term(first, last):
        exchange(term_send, term_recv, 3, first, last)

    send_term(1, 6)
    arrived(mix_recv, 2)


    put_rows(mix_recv)
    mixed = rows_wide[...]
    partial = dot_tn(mixed, grad_branch[...])
    gw_send[...] = partial[0:INNER, :].reshape(72, 8, MODEL).astype(BF16)
    for i in (2, 1, 3, 0):
        part = lax.rem(x + i, 4)
        remote(
            gw_send.at[pl.ds(36 * (1 - c) + 9 * part, 9)],
            gw_core.at[pl.ds(9 * part, 9)],
            red_send.at[0],
            core_part_recv.at[part],
            at(x, y, z, 1 - c),
        ).start()
    send_term(6, 10)
    branch = dot_nn(mixed, time_out[...])
    out_ref[...] = (hidden_rows[...].astype(F32) + gate_row * branch).astype(BF16)
    mod_sum[2:3, 0:MODEL] = jnp.sum(cotangent[...].astype(F32) * branch, axis=0, keepdims=True)
    for i in range(1, 4):
        remote(mod_sum, mod_y.at[i - 1], red_send.at[6], red_recv.at[6], at(x, y + i, z, c)).start()

    for i in (2, 1, 3, 0):
        part = lax.rem(x + i, 4)
        rows9 = pl.ds(9 * part, 9)
        wait_bytes(gw_core.at[rows9], core_part_recv.at[part])
        gw_half[rows9] = (
            gw_send[pl.ds(36 * c + 9 * part, 9)].astype(F32) + gw_core[rows9].astype(F32)
        ).astype(BF16)
        if i:

            @pl.when(c == 0)
            def _():
                remote(
                    gw_half.at[rows9], gw_x.at[i - 1], red_send.at[1], red_recv.at[1], at(part, y, z, c)
                ).start()

    own_cols = pl.ds(pl.multiple_of(256 * y, 128), 384)
    own_rows = pl.ds(9 * x, 9)

    def total_of(mine, others):
        total = mine.astype(F32)
        for i in range(3):
            total = total + others[i].astype(F32)
        return total.astype(BF16)

    def to_y(source, target, send, recv):
        for i in (2, 1, 3):
            to = lax.rem(y + i, 4)
            cols = pl.ds(pl.multiple_of(256 * to, 128), 384)
            remote(source.at[:, :, cols], target.at[i - 1], send, recv, at(x, to, z, c)).start()

    @pl.when(c == 1)
    def _():
        to_y(gw_half, gw_y1, red_send.at[1], red_recv.at[1])

    send_term(10, 16)

    wait_bytes(mod_y, red_recv.at[6])
    mod_tile[...] = mod_sum[...] + mod_y[0] + mod_y[1] + mod_y[2]
    for i in range(1, 8):
        to = lax.rem(zl + i, 8)
        block = (36 * (8 * y + to)) // 128
        col = pl.multiple_of(block * 128, 128)
        remote(
            mod_tile.at[:, pl.ds(col, 256)], mod_z.at[i - 1], red_send.at[7], red_recv.at[7], (dp, 8 * y + to)
        ).start()

    @pl.when(c == 0)
    def _():
        wait_bytes(gw_x, red_recv.at[1])
        gw_part[...] = total_of(gw_half[own_rows], gw_x)
        to_y(gw_part, gw_y, red_send.at[2], red_recv.at[2])
        send_term(16, 21)
        wait_bytes(gw_y, red_recv.at[2])
        gw_tile[...] = total_of(gw_part[:, :, own_cols], gw_y)

    @pl.when(c == 1)
    def _():
        wait_bytes(gw_y1, red_recv.at[1])
        gw_part1[...] = total_of(gw_half[:, :, own_cols], gw_y1)
        for i in (2, 1, 3):
            to = lax.rem(x + i, 4)
            remote(
                gw_part1.at[pl.ds(9 * to, 9)], gw_y.at[i - 1], red_send.at[2], red_recv.at[2], at(to, y, z, c)
            ).start()
        send_term(16, 21)
        wait_bytes(gw_y, red_recv.at[2])
        gw_tile[...] = total_of(gw_part1[own_rows], gw_y)

    for group in range(9):

        @pl.when(z != group)
        def _():
            remote(
                gw_tile.at[group], gw_z.at[z], red_send.at[3], red_recv.at[3], at(x, y, jnp.int32(group), c)
            ).start()

    send_term(21, 26)
    @pl.when(z < 9)
    def _():
        wait_bytes(gw_z.at[pl.ds(0, 15)], red_recv.at[3])
        gw_z[pl.ds(z, 1)] = gw_tile[pl.ds(z, 1)]
        total = jnp.sum(gw_z[...].astype(F32), axis=0)
        for place_z in range(8):
            turned = pltpu.roll(total, 384 - (32 * y + 36 * place_z), 1)
            gw_red[place_z] = turned[:, 0:128].astype(BF16)
        gw_all[pl.ds(z, 1)] = gw_red[pl.ds(zl, 1)]

        def send(i, carry):
            remote(
                gw_red.at[lax.rem(zl + i, 8)], gw_all.at[z], red_send.at[4], red_recv.at[4], at(x, y, z + i, c)
            ).start()
            return carry

        lax.fori_loop(1, 16, send, 0)

    send_term(26, SEQ)
    arrived(term_recv, 3)
    grad_hidden = (
        cotangent[...].astype(F32) + term_recv[...].astype(F32).reshape(ROWS, MODEL)
    ).astype(BF16)
    grad_attended = dot_nt(grad_hidden, cross_out[...]).astype(BF16)
    acc[...] = jnp.zeros_like(acc)

    def back(head):
        low, high = window(head)
        mask = head_mask(head)
        soft = probs_c[head]
        grad_soft = dot_nt(grad_attended[:, low:high], values[:, low:high] * mask)
        delta = jnp.sum(soft * grad_soft, axis=1, keepdims=True)
        grad_scores = (soft * (grad_soft - delta) * HEAD_SCALE).astype(BF16)
        acc[:, low:high] += dot_nn(grad_scores, keys[:, low:high] * mask)

    for head in range(4):
        back(head)

    @pl.when(z < 9)
    def _():
        wait_bytes(gw_all.at[pl.ds(0, 8)], red_recv.at[4])

    @pl.when(z >= 9)
    def _():
        wait_bytes(gw_all, red_recv.at[4])

    gw_last[pl.ds(u, 1)] = gw_all[...].reshape(1, 9, 8, 128)
    for i in range(1, 8):
        peer = lax.rem(x * 2 + c + i, 8)
        remote(
            gw_all, gw_last.at[u], red_send.at[5], red_recv.at[5], at(peer // 2, y, z, peer % 2)
        ).start()

    for head in range(4, HEADS):
        back(head)
    grad_latents[...] = (
        grad_hidden.astype(F32) + dot_nt(acc[...].astype(BF16), wa[:, 1152:1792])
    ).astype(BF16)

    wait_bytes(mod_z, red_recv.at[7])
    block = (36 * s) // 128
    mod_total = mod_tile[:, pl.ds(pl.multiple_of(block * 128, 128), 256)]
    for i in range(7):
        mod_total = mod_total + mod_z[i]
    mod_total = pltpu.roll(mod_total, lax.rem(256 - (36 * s - 128 * block), 256), 1)
    for i in range(3):
        grad_mod[i] = mod_total[i : i + 1, 0:36] * (SEQ * ROWS) ** (-0.5)

    wait_bytes(gw_last.at[pl.ds(0, 7)], red_recv.at[5])
    total = jnp.transpose(gw_last[...].astype(F32).reshape(INNER, 128))
    grad_weight[...] = total[0:36, :] * (SEQ * ROWS * 16) ** (-0.5)

    wait_bytes(z_recv.at[pl.ds(0, 7), pl.ds(0, 128)], zs_send.at[0])
    wait_bytes(z_recv.at[pl.ds(0, 7), pl.ds(128, 48)], zs_send.at[1])
    for k in order:
        if k == RB:
            wait_bytes(wa.at[pl.ds(0, 144), pl.ds(0, 128 * 15)], ring_send.at[k])
        else:
            wait_bytes(pieces_like(k, 15), ring_send.at[k])
        wait_bytes(core_part(k, c), core_send.at[k])
    for index, ref in ((0, gm_recv), (1, latent_recv), (2, mix_recv), (3, term_recv), (4, att_recv)):
        wait_bytes(ref.at[pl.ds(0, 31)], all_send.at[index])
    wait_bytes(gw_core, red_send.at[0])
    wait_bytes(gw_y, red_send.at[2])

    @pl.when(c == 0)
    def _():
        wait_bytes(gw_x, red_send.at[1])

    @pl.when(c == 1)
    def _():
        wait_bytes(gw_y1, red_send.at[1])


    @pl.when(z < 9)
    def _():
        wait_bytes(gw_z.at[pl.ds(0, 8)], red_send.at[3])
        wait_bytes(gw_z.at[pl.ds(0, 15), :, pl.ds(0, 128)], red_send.at[4])

    @pl.when(z >= 9)
    def _():
        wait_bytes(gw_z.at[pl.ds(0, 9)], red_send.at[3])

    wait_bytes(gw_last.at[pl.ds(0, 7)], red_send.at[5])
    wait_bytes(mod_y, red_send.at[6])
    wait_bytes(mod_z, red_send.at[7])


def body(
    latents,
    caption,
    caption_len,
    modulation,
    cross_query,
    cross_keyval,
    cross_output,
    time_qkv,
    time_output,
    cotangent,
):
    vmem = pl.BlockSpec(memory_space=pltpu.VMEM)
    sems = pltpu.SemaphoreType.DMA
    out, grad_in, grad_mod, grad_w = pl.pallas_call(
        kernel,
        out_shape=(
            jax.ShapeDtypeStruct((ROWS, MODEL), BF16),
            jax.ShapeDtypeStruct((ROWS, MODEL), BF16),
            jax.ShapeDtypeStruct((3, 1, 36), F32),
            jax.ShapeDtypeStruct((36, INNER), F32),
        ),
        in_specs=[vmem] * 7 + [pl.BlockSpec(memory_space=pltpu.SMEM)] + [vmem] * 2,
        out_specs=(vmem,) * 4,
        scratch_shapes=[
            pltpu.VMEM((40, 3456), F32),
            pltpu.VMEM((24, 2304), F32),
            pltpu.VMEM((40, 1792), F32),
            pltpu.VMEM((40, 128), F32),
            pltpu.VMEM((176, 128), F32),
            pltpu.VMEM((176, 128), BF16),
            pltpu.VMEM((8, 176, 128), BF16),
            pltpu.VMEM((8, 176, 128), F32),
            pltpu.VMEM((1584, 128), F32),
            pltpu.VMEM((1296, 128), BF16),
            pltpu.VMEM((304, MODEL), F32),
            pltpu.VMEM((ROWS, MODEL), BF16),
            pltpu.VMEM((ROWS, WIDE), BF16),
            pltpu.VMEM((SEQ, 8, MODEL), BF16),
            pltpu.VMEM((SEQ, 8, INNER), BF16),
            pltpu.VMEM((SEQ, 8, INNER), BF16),
            pltpu.VMEM((MODEL, 4096), BF16),
            pltpu.VMEM((INNER, 1024), BF16),
            pltpu.VMEM((WIDE, MODEL), BF16),
            pltpu.VMEM((WIDE, MODEL), BF16),
            pltpu.VMEM((SLOTS, WIDE), BF16),
            pltpu.VMEM((SLOTS, WIDE), BF16),
            pltpu.VMEM((ROWS, WIDE), BF16),
            pltpu.VMEM((HEADS, ROWS, SLOTS), F32),
            pltpu.VMEM((ROWS, WIDE), F32),
            pltpu.VMEM((ROWS, MODEL), BF16),
            pltpu.VMEM((SEQ, 8, INNER), BF16),
            pltpu.VMEM((SEQ, 8, INNER), BF16),
            pltpu.VMEM((SEQ, 8, INNER), BF16),
            pltpu.VMEM((SEQ, 8, INNER), BF16),
            pltpu.VMEM((SEQ, 8, MODEL), BF16),
            pltpu.VMEM((SEQ, 8, MODEL), BF16),
            pltpu.VMEM((ROWS, MODEL), F32),
            pltpu.VMEM((3, ROWS, WIDE), BF16),
            pltpu.VMEM((HEADS, ROWS, ROWS), F32),
            pltpu.VMEM((ROWS, MODEL), BF16),
            pltpu.VMEM((72, 8, MODEL), BF16),
            pltpu.VMEM((36, 8, MODEL), BF16),
            pltpu.VMEM((36, 8, MODEL), BF16),
            pltpu.VMEM((3, 9, 8, MODEL), BF16),
            pltpu.VMEM((9, 8, MODEL), BF16),
            pltpu.VMEM((3, 36, 8, 384), BF16),
            pltpu.VMEM((36, 8, 384), BF16),
            pltpu.VMEM((3, 9, 8, 384), BF16),
            pltpu.VMEM((9, 8, 384), BF16),
            pltpu.VMEM((16, 8, 384), BF16),
            pltpu.VMEM((8, 8, 128), BF16),
            pltpu.VMEM((9, 8, 128), BF16),
            pltpu.VMEM((8, 9, 8, 128), BF16),
            pltpu.VMEM((8, 1280), F32),
            pltpu.VMEM((3, 8, 1280), F32),
            pltpu.VMEM((8, 1280), F32),
            pltpu.VMEM((7, 8, 256), F32),
            sems((2,)),
            sems((2,)),
            sems((5,)),
            sems((5, 4)),
            sems((5, 4)),
            sems((5,)),
            sems((5,)),
            sems((5,)),
            sems((5,)),
            sems((5,)),
            sems((8,)),
            sems((8,)),
            sems((4,)),
        ],
        compiler_params=pltpu.CompilerParams(
            collective_id=0, has_side_effects=True, vmem_limit_bytes=60 * 2**20
        ),
    )(
        cross_query,
        cross_keyval,
        cross_output,
        time_qkv,
        time_output,
        latents.reshape(SEQ, 8, MODEL),
        caption[0],
        caption_len,
        jnp.swapaxes(modulation, 0, 1),
        cotangent.reshape(ROWS, MODEL),
    )
    return (
        out.reshape(latents.shape),
        grad_in.reshape(latents.shape),
        jnp.swapaxes(grad_mod, 0, 1),
        jnp.swapaxes(grad_w, 0, 1),
    )


def solution(mesh):
    placed = (
        P("dp", "seq", None, None),
        P("dp", None, None),
        P("dp"),
        P("dp", None, None),
        P("seq", None),
        P("seq", None),
        P("seq", None),
        P("seq", None),
        P("seq", None),
        P("dp", "seq", None, None),
    )
    return jax.shard_map(
        body,
        mesh=mesh,
        in_specs=placed,
        out_specs=(
            P("dp", "seq", None, None),
            P("dp", "seq", None, None),
            P("dp", None, "seq"),
            P(None, "seq"),
        ),
        check_vma=False,
    )
```
